32 devices in a mesh: dp: 4 (over y, x), ctx: 8 (over z, core).
Axes of the slice: x: 2, y: 2, z: 4, core: 2. Of those that a mesh axis runs over, the one named last changes fastest.
Arguments:
- tokens: bfloat16 [4, 2048, 4096], P('dp', 'ctx'), may hold values from -6 to 6
- queries: bfloat16 [4, 2048, 2048], P('dp', 'ctx'), may hold values from -260 to 260, as said below
- kv_weight: bfloat16 [4096, 1024], P('ctx', 'dp'), may hold values from -0.09375 to 0.09375
- doc_blocks: int32 [4, 4], P('dp'), may hold values from 1 to 8, 16 in all within a row
- block_mask: int32 [4, 16, 7], P('dp'), may hold values 0 or 1
- plan: int32 [4, 16], P('dp'), may hold values from 0 to 15, as said below
Outputs:
- attended: bfloat16 [4, 2048, 2048], P('dp', 'ctx')
- stats: float32 [4, 16, 2048], P('dp', None, 'ctx')
The draws below stay inside these ranges and needn't reach their ends.
Inputs may be any that keep to these rules, and one draw needn't show every extreme that they name: queries of unit order, in some draws with a few rows far larger. `doc_blocks`: the documents of a pack in order, their lengths summing to 16. `block_mask`: entry [b, w] lets block b attend block b - w - 1 where that block is of the same document. plan[b] = ctx index * 2 + place; the slot lies on block b's own ctx index or on the one that differs from it in the lowest bit, and every slot is named by exactly one block.
All inputs are finite; a program needn't handle non-finite values.
Results may differ from the reference program's by a relative error of at most 0.012.
The reference program's roundings to bfloat16 on the way count: a program that leaves them out, or rounds other values in their place, can miss the bound.
Values may be sent and summed in bfloat16 or wider, within the bound.
No kernel may reach another device: no remote copies, remote signals or barrier semaphores. Data moves between devices by JAX's collectives and lax.ppermute only.
A program may use at most 128 MiB of HBM per device.

```python
import math
import jax
import jax.numpy as jnp
import numpy as np
from jax import lax

D = 4096
HD = 128
QH = 16
KVH = 4
BLK = 128
MAXDOC = 8
BDEV = 2
PACKS = 4
NB = 16
PACK = 2048
NDOC = 4
KVW = 1024


def draw_queries(key, part):
    shape = (PACKS, NB * BLK, QH * HD)
    first = jax.random.fold_in(key, 0)
    return jnp.clip(jax.random.normal(first, shape, jnp.float32), -4.0, 4.0).astype(jnp.bfloat16)


def draw_plan(key, part):
    group = 2 * BDEV
    count = NB // group

    def one_pack(pack_key):
        scores = jax.random.randint(pack_key, (count, group), 0, 1 << 20)
        scores = scores * group + jnp.arange(group, dtype=jnp.int32)[None, :]
        order = jnp.argsort(scores, axis=1).astype(jnp.int32)
        offsets = (jnp.arange(count, dtype=jnp.int32) * group)[:, None]
        return (offsets + order).reshape(NB).astype(jnp.int32)
    return jax.vmap(one_pack)(jax.random.split(key, PACKS))


def with_ends(drawn, stream_key, least, high):
    dims = drawn.shape
    spot = [jax.random.randint(jax.random.fold_in(stream_key, axis), (), 0, dims[axis]) for axis in range(len(dims))]
    drawn = drawn.at[tuple(spot)].set(least)
    longest = dims.index(max(dims))
    spot[longest] = (spot[longest] + 1) % dims[longest]
    return drawn.at[tuple(spot)].set(high)


def block_levels(rng, dims, cuts, low, largest):
    def one(dim, blocks):
        draws = jax.random.uniform(jax.random.fold_in(jax.random.fold_in(rng, 6), dim), (blocks,), jnp.float32, low / len(cuts), largest / len(cuts))
        return jnp.repeat(jnp.exp(draws), dims[dim] // blocks).reshape((-1,) + (1,) * (len(dims) - dim - 1))

    factor_of = one(*cuts[0])
    for cut in cuts[1:]:
        factor_of = factor_of * one(*cut)
    return factor_of


def length_profile(number_of, total, reach, lean):
    loads = [(1 << 20) // math.isqrt(grade ** lean) + 1 for grade in range(2, number_of + 1)]
    rest, holding = total - reach - (number_of - 1), [1] * (number_of - 1)
    while rest > 0:
        movable = [i for i in range(number_of - 1) if holding[i] < reach]
        pool, budget = sum([loads[i] for i in movable]), rest
        for i in movable:
            more = min(reach - holding[i], max(1, budget * loads[i] // pool), rest)
            holding[i] = holding[i] + more
            rest = rest - more
    return np.array([reach] + holding)


def ragged_sizes(stream_key, amount, total, limit, lean):
    if amount == 2:
        one = jax.random.randint(stream_key, (), max(1, total - limit), min(limit, total - 1) + 1)
        return jnp.stack([one, total - one])
    lengths = jnp.asarray(length_profile(amount, total, limit, lean), jnp.int32)
    twos = (amount - 1) // 2
    giver, sink = lengths[1:1 + 2 * twos:2], lengths[2:2 + 2 * twos:2]
    room = jnp.minimum(giver - 1, limit - sink)
    passed = jax.random.randint(jax.random.fold_in(stream_key, 1), (twos,), 0, 1 << 20) % (room + 1)
    lengths = lengths.at[1:1 + 2 * twos:2].set(giver - passed).at[2:2 + 2 * twos:2].set(sink + passed)
    return lengths[jax.random.permutation(jax.random.fold_in(stream_key, 2), amount)]


def normal_values(own_key, dims, scale, limit, cuts=(), held_as=jnp.bfloat16):
    gain = block_levels(own_key, dims, cuts, -0.22, 0.18) if cuts else 1.0
    values = jax.random.normal(own_key, dims, jnp.float32) * scale * gain
    return jnp.minimum(jnp.maximum(values, -limit), limit).astype(held_as)


def setup_inputs(seed: int = 0) -> dict:
    seeds = jax.random.split(jax.random.key(seed), 7)
    tokens = normal_values(seeds[0], (PACKS, PACK, D), 1.0, 6.0, ((0, 4), (1, 8)))
    queries = draw_queries(jax.random.fold_in(seeds[6], 71), 0)
    kv_weight = normal_values(seeds[2], (D, KVW), D ** -0.5, 0.09375, ((0, 8), (1, 4)))
    doc_blocks = jax.vmap(lambda own: ragged_sizes(own, NDOC, NB, MAXDOC, 2))(jax.random.split(seeds[3], PACKS)).reshape((PACKS, NDOC)).astype(jnp.int32)
    block_mask = with_ends((jax.random.randint(seeds[4], (PACKS, NB, MAXDOC - 1), 0, 4) < 3).astype(jnp.int32), jax.random.fold_in(seeds[4], 1), 0, 1)
    plan = draw_plan(jax.random.fold_in(seeds[6], 71), 0)
    return {"tokens": tokens, "queries": queries, "kv_weight": kv_weight, "doc_blocks": doc_blocks, "block_mask": block_mask, "plan": plan}


def document_of_blocks(doc_blocks):
    ends = jnp.cumsum(doc_blocks).astype(jnp.int32)
    blocks = jnp.arange(NB, dtype=jnp.int32)
    return lax.optimization_barrier(jnp.sum((blocks[:, None] >= ends[None, :]).astype(jnp.int32), axis=1)).astype(jnp.int32)

def attend_pack(tokens, queries, kv_weight, doc_blocks, block_mask, plan):
    group = QH // KVH
    width = 2 * KVH * HD
    pairs = jnp.dot(tokens, kv_weight, preferred_element_type=jnp.float32).astype(jnp.bfloat16)
    pairs = pairs.reshape(NB, BLK, width)
    padded = jnp.concatenate([jnp.zeros((MAXDOC - 1, BLK, width), jnp.bfloat16), pairs], axis=0)
    documents = document_of_blocks(doc_blocks)
    padded_docs = jnp.concatenate([jnp.full((MAXDOC - 1,), -1, jnp.int32), documents])
    heads = queries.reshape(NB, BLK, KVH, group, HD)
    places = jnp.arange(BLK, dtype=jnp.int32)
    causal = places[None, :] <= places[:, None]
    last = jnp.arange(MAXDOC, dtype=jnp.int32) == MAXDOC - 1
    token_keep = jnp.logical_or(jnp.logical_not(last)[:, None, None], causal[None])
    scale = 1.0 / math.sqrt(HD)

    def one_block(index):
        window = lax.dynamic_slice_in_dim(padded, index, MAXDOC, 0)
        window_docs = lax.dynamic_slice_in_dim(padded_docs, index, MAXDOC, 0)
        gates = jnp.concatenate([block_mask[index][::-1], jnp.ones((1,), jnp.int32)])
        allowed = (window_docs == documents[index]) & (gates == 1)
        keys = window[:, :, :KVH * HD].reshape(MAXDOC * BLK, KVH, HD).astype(jnp.float32)
        values = window[:, :, KVH * HD:].reshape(MAXDOC * BLK, KVH, HD).astype(jnp.float32)
        query = heads[index].astype(jnp.float32)
        scores = jnp.einsum('ikgd,lkd->kgil', query, keys) * scale
        keep = (allowed[:, None, None] & token_keep).transpose(1, 0, 2).reshape(BLK, MAXDOC * BLK)
        scores = jnp.where(keep[None, None], scores, -jnp.inf)
        rowmax = lax.optimization_barrier(jnp.max(scores, axis=-1, keepdims=True))
        weights = jnp.exp(scores - rowmax)
        total = lax.optimization_barrier(jnp.sum(weights, axis=-1))
        rounded = lax.optimization_barrier(weights.astype(jnp.bfloat16)).astype(jnp.float32)
        summed = jnp.einsum('kgil,lkd->kgid', rounded, values)
        out = (summed / total[..., None]).transpose(2, 0, 1, 3).reshape(BLK, QH * HD).astype(jnp.bfloat16)
        stats = (rowmax[..., 0] + jnp.log(total)).reshape(QH, BLK)
        return (out, stats)
    outs, stats = lax.map(one_block, jnp.arange(NB, dtype=jnp.int32))
    placed = jnp.zeros_like(stats).at[plan].set(stats)
    return (outs.reshape(NB * BLK, QH * HD), placed.transpose(1, 0, 2).reshape(QH, NB * BLK))

def reference(tokens, queries, kv_weight, doc_blocks, block_mask, plan):
    results = [attend_pack(tokens[pack], queries[pack], kv_weight, doc_blocks[pack], block_mask[pack], plan[pack]) for pack in range(PACKS)]
    return (jnp.stack([item[0] for item in results]), jnp.stack([item[1] for item in results]))
```

```python
import functools
import math

import jax
import jax.numpy as jnp
from jax import lax
from jax.experimental import pallas as pl
from jax.experimental.pallas import tpu as pltpu
from jax.sharding import PartitionSpec as P

HD = 128
QH = 16
KVH = 4
BLK = 128
MAXDOC = 8
GROUP = QH // KVH
LANES = GROUP * BLK
VMEM_LIMIT = 48 * 1024 * 1024
SCALE = 1.0 / math.sqrt(HD)
LOG2E = 1.0 / math.log(2.0)


def over_dp(array, mask):
    return lax.ppermute(array, "dp", [(i, i ^ mask) for i in range(lax.axis_size("dp"))])


def other_core(array):
    return lax.ppermute(array, "ctx", [(i, i ^ 1) for i in range(lax.axis_size("ctx"))])


def around(array, pairs):
    size = lax.axis_size("ctx")
    return lax.ppermute(array, "ctx", [(i, (i + 2 * pairs) % size) for i in range(size)])


def ahead(array, pairs):
    size = lax.axis_size("ctx")
    return lax.ppermute(array, "ctx", [(i, i + 2 * pairs) for i in range(size - 2 * pairs)])


def project_kernel(slots, own_ref, other_ref, *refs):
    weights, out_ref = refs[:-1], refs[-1]
    device = lax.axis_index("ctx")
    core, pair = device % 2, device // 2
    rows = own_ref.shape[0]
    depth = weights[0].shape[0] // 2
    for tokens_ref, place in ((own_ref, core), (other_ref, 1 - core)):
        total = jnp.zeros((rows, HD), jnp.float32)
        for step, weight in enumerate(weights):
            source = lax.rem(pair + slots - step, slots)
            for half in range(2):
                group = 2 * source + (core + half) % 2
                columns = pl.ds(pl.multiple_of(group * depth, depth), depth)
                total += jnp.dot(
                    tokens_ref[:, columns],
                    weight[half * depth : (half + 1) * depth, :],
                    preferred_element_type=jnp.float32,
                )
        out_ref[pl.ds(pl.multiple_of(place * rows, rows), rows), :] = total.astype(jnp.bfloat16)


def project(own, other, weights):
    rows, width = own.shape
    spec = pl.BlockSpec(memory_space=pltpu.VMEM)
    return pl.pallas_call(
        functools.partial(project_kernel, len(weights)),
        out_shape=jax.ShapeDtypeStruct((2 * rows, HD), jnp.bfloat16),
        in_specs=[spec] * (2 + len(weights)),
        out_specs=spec,
        compiler_params=pltpu.CompilerParams(vmem_limit_bytes=VMEM_LIMIT),
        cost_estimate=pl.CostEstimate(
            flops=8 * rows * width * HD, bytes_accessed=4 * rows * width, transcendentals=0
        ),
    )(own, other, *weights)


def attend_kernel(
    second,
    docs_ref,
    mask_ref,
    plan_ref,
    q_own_ref,
    q_other_ref,
    near_a,
    near_b,
    back_a,
    back_b,
    far_a,
    far_b,
    out_own,
    out_other,
    stats_own,
    stats_other,
    kv,
    table,
    top,
    total,
    summed,
):
    device = lax.axis_index("ctx")
    slice_of = lax.axis_index("dp")
    core, pair = device % 2, device // 2
    column, kind = slice_of % 2, slice_of // 2
    head_pair = (column + second) % 2
    head = 2 * head_pair + core
    pair_blocks = near_a.shape[0] // BLK
    far_blocks = far_a.shape[0] // BLK
    dev_blocks = pair_blocks // 2
    count = plan_ref.shape[1]
    documents = docs_ref.shape[1]
    first = pair * pair_blocks
    own_row = (far_blocks + pair_blocks) * BLK
    for which, near, back, far in ((kind, near_a, back_a, far_a), (1 - kind, near_b, back_b, far_b)):
        kv[which, : far_blocks * BLK, :] = far[...]
        kv[which, far_blocks * BLK : own_row, :] = back[...]
        kv[which, own_row:, :] = near[...]
    causal = lax.broadcasted_iota(jnp.int32, (BLK, BLK), 0) <= lax.broadcasted_iota(
        jnp.int32, (BLK, BLK), 1
    )
    columns = pl.ds(pl.multiple_of(head * LANES, LANES), LANES)

    for is_own, q_ref, out_ref in ((1, q_own_ref, out_own), (0, q_other_ref, out_other)):
        owner = core if is_own else 1 - core
        for place in range(dev_blocks):
            index = owner * dev_blocks + place
            block = first + index
            rows = slice(place * BLK, (place + 1) * BLK)
            query = q_ref[rows, columns]
            stacked = jnp.concatenate(
                [query[:, g * HD : (g + 1) * HD] for g in range(GROUP)], axis=0
            )

            def ends(j, carry):
                end, start = carry
                end = end + docs_ref[0, j]
                return end, jnp.where(end <= block, end, start)

            _, start = lax.fori_loop(0, documents, ends, (jnp.int32(0), jnp.int32(0)))

            def row_of(back):
                return pl.multiple_of(own_row + (index - back) * BLK, BLK)

            def scores(back):
                keys = kv[0, pl.ds(row_of(back), BLK), :]
                return lax.dot_general(
                    keys, stacked, (((1,), (1,)), ((), ())), preferred_element_type=jnp.float32
                )

            def admitted(back):
                return jnp.logical_and(block - back >= start, mask_ref[0, block, back - 1] == 1)

            own_scores = jnp.where(jnp.tile(causal, (1, GROUP)), scores(0), -jnp.inf)
            table[0] = own_scores
            top[...] = jnp.max(own_scores, axis=0, keepdims=True)
            for back in range(1, MAXDOC):

                @pl.when(admitted(back))
                def _():
                    got = scores(back)
                    table[back] = got
                    top[...] = jnp.maximum(top[...], jnp.max(got, axis=0, keepdims=True))

            def weigh(back):
                weights = jnp.exp2((table[back] - top[...]) * (SCALE * LOG2E))
                values = kv[1, pl.ds(row_of(back), BLK), :]
                part = lax.dot_general(
                    values,
                    weights.astype(jnp.bfloat16),
                    (((0,), (0,)), ((), ())),
                    preferred_element_type=jnp.float32,
                )
                return jnp.sum(weights, axis=0, keepdims=True), part

            total[...], summed[...] = weigh(0)
            for back in range(1, MAXDOC):

                @pl.when(admitted(back))
                def _():
                    more, part = weigh(back)
                    total[...] += more
                    summed[...] += part

            result = summed[...] / total[...]
            for g in range(GROUP):
                out_ref[rows, g * HD : (g + 1) * HD] = (
                    result[:, g * BLK : (g + 1) * BLK].T.astype(jnp.bfloat16)
                )
            lse = top[...] * SCALE + jnp.log(total[...])
            slot = plan_ref[0, block] - first
            keep_here = slot // dev_blocks == core
            at = slot % dev_blocks

            @pl.when(keep_here)
            def _():
                for g in range(GROUP):
                    stats_own[at, g : g + 1, :] = lse[:, g * BLK : (g + 1) * BLK]

            @pl.when(jnp.logical_not(keep_here))
            def _():
                for g in range(GROUP):
                    stats_other[at, g : g + 1, :] = lse[:, g * BLK : (g + 1) * BLK]


def attend(second, docs, mask, plan, q_own, q_other, first_set, second_set):
    vmem = pl.BlockSpec(memory_space=pltpu.VMEM)
    smem = pl.BlockSpec(memory_space=pltpu.SMEM)
    rows = q_own.shape[0]
    dev_blocks = rows // BLK
    near_a, back_a, far_a = first_set
    near_b, back_b, far_b = second_set
    window = near_a.shape[0] + back_a.shape[0] + far_a.shape[0]
    out = jax.ShapeDtypeStruct((rows, LANES), jnp.bfloat16)
    stats = jax.ShapeDtypeStruct((dev_blocks, GROUP, BLK), jnp.float32)
    return pl.pallas_call(
        functools.partial(attend_kernel, second),
        out_shape=(out, out, stats, stats),
        in_specs=[smem] * 3 + [vmem] * 8,
        out_specs=(vmem,) * 4,
        scratch_shapes=[
            pltpu.VMEM((2, window, HD), jnp.bfloat16),
            pltpu.VMEM((MAXDOC, BLK, LANES), jnp.float32),
            pltpu.VMEM((1, LANES), jnp.float32),
            pltpu.VMEM((1, LANES), jnp.float32),
            pltpu.VMEM((HD, LANES), jnp.float32),
        ],
        compiler_params=pltpu.CompilerParams(vmem_limit_bytes=VMEM_LIMIT),
        cost_estimate=pl.CostEstimate(
            flops=2 * dev_blocks * MAXDOC * BLK * LANES * HD * 4,
            bytes_accessed=8 * rows * QH * HD,
            transcendentals=2 * dev_blocks * MAXDOC * BLK * LANES,
        ),
    )(docs, mask, plan, q_own, q_other, near_a, near_b, back_a, back_b, far_a, far_b)


def finish_kernel(
    own_a, own_b, got_a, got_b, st_own_a, st_own_b, st_got_a, st_got_b, out_ref, stats_ref
):
    core = lax.axis_index("ctx") % 2
    column = lax.axis_index("dp") % 2
    pieces = (
        (own_a, column, core),
        (own_b, 1 - column, core),
        (got_a, column, 1 - core),
        (got_b, 1 - column, 1 - core),
    )
    for piece, head_pair, side in pieces:
        head = 2 * head_pair + side
        out_ref[0, :, pl.ds(pl.multiple_of(head * LANES, LANES), LANES)] = piece[...]
    for head in range(KVH):
        is_a = head // 2 == column
        is_own = head % 2 == core
        own = jnp.where(is_a, st_own_a[...], st_own_b[...])
        got = jnp.where(is_a, st_got_a[...], st_got_b[...])
        lse = jnp.where(is_own, own, got)
        for place in range(lse.shape[0]):
            stats_ref[0, head * GROUP : (head + 1) * GROUP, place * BLK : (place + 1) * BLK] = lse[place]


def body(tokens, queries, kv_weight, doc_blocks, block_mask, plan):
    size = lax.axis_size("ctx")
    device = lax.axis_index("ctx")
    core = device % 2
    slots = size // 2
    own_tokens, own_queries = tokens[0], queries[0]
    rows = own_tokens.shape[0]
    other_weight = other_core(kv_weight)
    other_tokens = other_core(own_tokens)
    other_queries = other_core(own_queries)

    def my_half(array):
        return lax.dynamic_slice_in_dim(array, core * HD, HD, 1)

    mine = my_half(kv_weight)
    others = my_half(other_weight)
    if slots == 4:
        slab = jnp.concatenate([mine, others], axis=0)
        own_set = [slab] + [around(slab, step) for step in (1, 2, 3)]

        def multiply(weights):
            return project(own_tokens, other_tokens, weights)

        x_set = [over_dp(w, 1) for w in own_set]
        y_set = [over_dp(w, 2) for w in own_set]
        d_set = [over_dp(x_set[0], 2), over_dp(y_set[1], 1), over_dp(x_set[2], 2), over_dp(y_set[3], 1)]
    else:
        even = jnp.where(core == 0, mine, others)
        odd = jnp.where(core == 0, others, mine)
        groups = [list(range(0, size, 2)), list(range(1, size, 2))]
        slab = jnp.concatenate([even, odd], axis=0)
        own_set = lax.all_gather(slab, "ctx", axis=0, axis_index_groups=groups, tiled=True)
        pair_tokens = jnp.where(
            core == 0,
            jnp.concatenate([own_tokens, other_tokens], axis=0),
            jnp.concatenate([other_tokens, own_tokens], axis=0),
        )

        def multiply(weights):
            total = jnp.dot(pair_tokens, weights, preferred_element_type=jnp.float32)
            return total.astype(jnp.bfloat16)

        x_set = over_dp(own_set, 1)
        y_set = over_dp(own_set, 2)
        d_set = over_dp(x_set, 2)

    spare = 2 * rows // BLK - (MAXDOC - 1) % (2 * rows // BLK)

    def reach(near):
        return near, ahead(near, 1), ahead(near[spare * BLK :], 2)

    own_kv = reach(multiply(own_set))
    y_kv = reach(multiply(y_set))
    x_kv = reach(multiply(x_set))
    d_kv = reach(multiply(d_set))
    first = attend(0, doc_blocks, block_mask, plan, own_queries, other_queries, own_kv, y_kv)
    second = attend(1, doc_blocks, block_mask, plan, own_queries, other_queries, x_kv, d_kv)
    got_a, got_b = other_core(first[1]), other_core(second[1])
    st_got_a, st_got_b = other_core(first[3]), other_core(second[3])
    vmem = pl.BlockSpec(memory_space=pltpu.VMEM)
    return pl.pallas_call(
        finish_kernel,
        out_shape=(
            jax.ShapeDtypeStruct((1, rows, QH * HD), jnp.bfloat16),
            jax.ShapeDtypeStruct((1, QH, rows), jnp.float32),
        ),
        in_specs=[vmem] * 8,
        out_specs=(vmem, vmem),
        compiler_params=pltpu.CompilerParams(vmem_limit_bytes=VMEM_LIMIT),
    )(first[0], second[0], got_a, got_b, first[2], second[2], st_got_a, st_got_b)


def solution(mesh):
    in_specs = (
        P("dp", "ctx", None),
        P("dp", "ctx", None),
        P("ctx", "dp"),
        P("dp", None),
        P("dp", None, None),
        P("dp", None),
    )
    out_specs = (P("dp", "ctx", None), P("dp", None, "ctx"))
    return jax.shard_map(body, mesh=mesh, in_specs=in_specs, out_specs=out_specs, check_vma=False)
```

```python
import functools
import math

import jax
import jax.numpy as jnp
from jax import lax
from jax.experimental import pallas as pl
from jax.experimental.pallas import tpu as pltpu
from jax.sharding import PartitionSpec as P

HD = 128
QH = 16
KVH = 4
BLK = 128
MAXDOC = 8
GROUP = QH // KVH
LANES = GROUP * BLK
VMEM_LIMIT = 48 * 1024 * 1024
SCALE = 1.0 / math.sqrt(HD)
LOG2E = 1.0 / math.log(2.0)
PAUSE = 50_000_000_000


def over_dp(array, mask):
    return lax.ppermute(array, "dp", [(i, i ^ mask) for i in range(lax.axis_size("dp"))])


def other_core(array):
    return lax.ppermute(array, "ctx", [(i, i ^ 1) for i in range(lax.axis_size("ctx"))])


def around(array, pairs):
    size = lax.axis_size("ctx")
    return lax.ppermute(array, "ctx", [(i, (i + 2 * pairs) % size) for i in range(size)])


def after(array, *others):
    return lax.optimization_barrier((array,) + others)[0]


def pause_kernel(token_ref, out_ref):
    out_ref[...] = token_ref[...]


def pause(token, *others):
    return pl.pallas_call(
        pause_kernel,
        out_shape=jax.ShapeDtypeStruct(token.shape, token.dtype),
        in_specs=[pl.BlockSpec(memory_space=pltpu.VMEM)],
        out_specs=pl.BlockSpec(memory_space=pltpu.VMEM),
        cost_estimate=pl.CostEstimate(flops=PAUSE, bytes_accessed=0, transcendentals=0),
    )(after(token, *others))


def project_kernel(slots, spare, own_ref, other_ref, *refs):
    sets = len(refs[:-2]) // slots
    weights, near_ref, far_ref = refs[:-2], refs[-2], refs[-1]
    device = lax.axis_index("ctx")
    core, pair = device % 2, device // 2
    rows = own_ref.shape[0]
    depth = weights[0].shape[0] // 2
    tall, short = 2 * rows, 2 * rows - spare
    for tokens_ref, place in ((own_ref, core), (other_ref, 1 - core)):
        total = jnp.zeros((rows, sets * HD), jnp.float32)
        for step in range(slots):
            source = lax.rem(pair + slots - step, slots)
            for half in range(2):
                group = 2 * source + (core + half) % 2
                columns = pl.ds(pl.multiple_of(group * depth, depth), depth)
                part = slice(half * depth, (half + 1) * depth)
                weight = jnp.concatenate(
                    [weights[s * slots + step][part, :] for s in range(sets)], axis=1
                )
                total += jnp.dot(
                    tokens_ref[:, columns], weight, preferred_element_type=jnp.float32
                )
        total = total.astype(jnp.bfloat16)
        for s in range(sets):
            near_ref[pl.ds(pl.multiple_of(s * tall + place * rows, rows), rows), :] = total[
                :, s * HD : (s + 1) * HD
            ]
    for s in range(sets):
        far_ref[s * short : (s + 1) * short, :] = near_ref[s * tall + spare : (s + 1) * tall, :]


def project(own, other, sets, spare):
    rows, width = own.shape
    weights = [w for one in sets for w in one]
    count = len(sets)
    spec = pl.BlockSpec(memory_space=pltpu.VMEM)
    return pl.pallas_call(
        functools.partial(project_kernel, len(sets[0]), spare),
        out_shape=(
            jax.ShapeDtypeStruct((count * 2 * rows, HD), jnp.bfloat16),
            jax.ShapeDtypeStruct((count * (2 * rows - spare), HD), jnp.bfloat16),
        ),
        in_specs=[spec] * (2 + len(weights)),
        out_specs=(spec, spec),
        compiler_params=pltpu.CompilerParams(vmem_limit_bytes=VMEM_LIMIT),
        cost_estimate=pl.CostEstimate(
            flops=8 * rows * width * HD * count,
            bytes_accessed=4 * rows * width,
            transcendentals=0,
        ),
    )(own, other, *weights)


def attend_kernel(
    second,
    at_a,
    at_b,
    docs_ref,
    mask_ref,
    plan_ref,
    q_own_ref,
    q_other_ref,
    near_a,
    near_b,
    back_a,
    back_b,
    far_a,
    far_b,
    out_own,
    out_other,
    stats_own,
    stats_other,
    kv,
    table,
    top,
    total,
    summed,
    places,
):
    device = lax.axis_index("ctx")
    slice_of = lax.axis_index("dp")
    core, pair = device % 2, device // 2
    column, kind = slice_of % 2, slice_of // 2
    head_pair = (column + second) % 2
    head = 2 * head_pair + core
    dev_blocks = q_own_ref.shape[0] // BLK
    pair_blocks = 2 * dev_blocks
    far_blocks = (MAXDOC - 1) % pair_blocks
    count = plan_ref.shape[1]
    documents = docs_ref.shape[1]
    first = pair * pair_blocks
    own_row = (far_blocks + pair_blocks) * BLK
    tall, short = pair_blocks * BLK, far_blocks * BLK
    for which, at, near, back, far in (
        (kind, at_a, near_a, back_a, far_a),
        (1 - kind, at_b, near_b, back_b, far_b),
    ):
        kv[which, :short, :] = far[at * short : (at + 1) * short, :]
        kv[which, short:own_row, :] = back[at * tall : (at + 1) * tall, :]
        kv[which, own_row:, :] = near[at * tall : (at + 1) * tall, :]
    causal = lax.broadcasted_iota(jnp.int32, (BLK, BLK), 0) <= lax.broadcasted_iota(
        jnp.int32, (BLK, BLK), 1
    )
    causal = jnp.tile(causal, (1, GROUP))
    columns = pl.ds(pl.multiple_of(head * LANES, LANES), LANES)

    for is_own, q_ref, out_ref in ((1, q_own_ref, out_own), (0, q_other_ref, out_other)):
        owner = core if is_own else 1 - core
        for place in range(dev_blocks):
            index = owner * dev_blocks + place
            block = first + index
            rows = slice(place * BLK, (place + 1) * BLK)

            def ends(j, carry):
                end, start = carry
                end = end + docs_ref[0, j]
                return end, jnp.where(end <= block, end, start)

            _, start = lax.fori_loop(0, documents, ends, (jnp.int32(0), jnp.int32(0)))
            for back in range(MAXDOC):
                places[back] = own_row + index * BLK
            found = jnp.int32(1)
            for back in range(1, MAXDOC):
                places[found] = own_row + (index - back) * BLK
                admitted = jnp.logical_and(
                    block - back >= start, mask_ref[0, block, back - 1] == 1
                )
                found += admitted.astype(jnp.int32)

            query = q_ref[rows, columns]
            stacked = jnp.concatenate(
                [query[:, g * HD : (g + 1) * HD] for g in range(GROUP)], axis=0
            )

            def fetch(which, step):
                return kv[which, pl.ds(pl.multiple_of(places[step], BLK), BLK), :]

            def score(steps):
                best = None
                for step in steps:
                    got = lax.dot_general(
                        fetch(0, step),
                        stacked,
                        (((1,), (1,)), ((), ())),
                        preferred_element_type=jnp.float32,
                    )
                    got = jnp.where(causal if step == 0 else step < found, got, -jnp.inf)
                    table[step * BLK : (step + 1) * BLK, :] = got
                    best = got if best is None else jnp.maximum(best, got)
                return jnp.max(best, axis=0, keepdims=True)

            def weigh(steps, highest):
                weights = jnp.exp2(
                    (table[steps[0] * BLK : (steps[-1] + 1) * BLK, :] - highest) * (SCALE * LOG2E)
                )
                values = jnp.concatenate([fetch(1, step) for step in steps], axis=0)
                part = lax.dot_general(
                    values,
                    weights.astype(jnp.bfloat16),
                    (((0,), (0,)), ((), ())),
                    preferred_element_type=jnp.float32,
                )
                return jnp.sum(weights, axis=0, keepdims=True), part

            half = MAXDOC // 2
            top[...] = score(range(half))

            @pl.when(found > half)
            def _():
                top[...] = jnp.maximum(top[...], score(range(half, MAXDOC)))

            total[...], summed[...] = weigh(range(half), top[...])

            @pl.when(found > half)
            def _():
                more, part = weigh(range(half, MAXDOC), top[...])
                total[...] += more
                summed[...] += part

            result = summed[...] / total[...]
            for g in range(GROUP):
                out_ref[rows, g * HD : (g + 1) * HD] = (
                    result[:, g * BLK : (g + 1) * BLK].T.astype(jnp.bfloat16)
                )
            lse = top[...] * SCALE + jnp.log(total[...])
            slot = plan_ref[0, block] - first
            keep_here = slot // dev_blocks == core
            at = slot % dev_blocks

            @pl.when(keep_here)
            def _():
                for g in range(GROUP):
                    stats_own[at, g : g + 1, :] = lse[:, g * BLK : (g + 1) * BLK]

            @pl.when(jnp.logical_not(keep_here))
            def _():
                for g in range(GROUP):
                    stats_other[at, g : g + 1, :] = lse[:, g * BLK : (g + 1) * BLK]


def attend(second, docs, mask, plan, q_own, q_other, first_set, second_set):
    vmem = pl.BlockSpec(memory_space=pltpu.VMEM)
    smem = pl.BlockSpec(memory_space=pltpu.SMEM)
    rows = q_own.shape[0]
    dev_blocks = rows // BLK
    at_a, near_a, back_a, far_a = first_set
    at_b, near_b, back_b, far_b = second_set
    window = (4 * dev_blocks + (MAXDOC - 1) % (2 * dev_blocks)) * BLK
    out = jax.ShapeDtypeStruct((rows, LANES), jnp.bfloat16)
    stats = jax.ShapeDtypeStruct((dev_blocks, GROUP, BLK), jnp.float32)
    return pl.pallas_call(
        functools.partial(attend_kernel, second, at_a, at_b),
        out_shape=(out, out, stats, stats),
        in_specs=[smem] * 3 + [vmem] * 8,
        out_specs=(vmem,) * 4,
        scratch_shapes=[
            pltpu.VMEM((2, window, HD), jnp.bfloat16),
            pltpu.VMEM((MAXDOC * BLK, LANES), jnp.float32),
            pltpu.VMEM((1, LANES), jnp.float32),
            pltpu.VMEM((1, LANES), jnp.float32),
            pltpu.VMEM((HD, LANES), jnp.float32),
            pltpu.SMEM((MAXDOC + 1,), jnp.int32),
        ],
        compiler_params=pltpu.CompilerParams(vmem_limit_bytes=VMEM_LIMIT),
        cost_estimate=pl.CostEstimate(
            flops=2 * dev_blocks * MAXDOC * BLK * LANES * HD * 4,
            bytes_accessed=8 * rows * QH * HD,
            transcendentals=2 * dev_blocks * MAXDOC * BLK * LANES,
        ),
    )(docs, mask, plan, q_own, q_other, near_a, near_b, back_a, back_b, far_a, far_b)


def finish_kernel(
    own_a, own_b, got_a, got_b, st_own_a, st_own_b, st_got_a, st_got_b, out_ref, stats_ref
):
    core = lax.axis_index("ctx") % 2
    column = lax.axis_index("dp") % 2
    pieces = (
        (own_a, column, core),
        (own_b, 1 - column, core),
        (got_a, column, 1 - core),
        (got_b, 1 - column, 1 - core),
    )
    for piece, head_pair, side in pieces:
        head = 2 * head_pair + side
        out_ref[0, :, pl.ds(pl.multiple_of(head * LANES, LANES), LANES)] = piece[...]
    for head in range(KVH):
        is_a = head // 2 == column
        is_own = head % 2 == core
        own = jnp.where(is_a, st_own_a[...], st_own_b[...])
        got = jnp.where(is_a, st_got_a[...], st_got_b[...])
        lse = jnp.where(is_own, own, got)
        for place in range(lse.shape[0]):
            stats_ref[0, head * GROUP : (head + 1) * GROUP, place * BLK : (place + 1) * BLK] = lse[place]


def body(tokens, queries, kv_weight, doc_blocks, block_mask, plan):
    size = lax.axis_size("ctx")
    device = lax.axis_index("ctx")
    core = device % 2
    slots = size // 2
    own_tokens, own_queries = tokens[0], queries[0]
    rows = own_tokens.shape[0]
    other_weight = other_core(kv_weight)
    other_tokens = other_core(after(own_tokens, other_weight))
    other_queries = other_core(after(own_queries, other_weight))

    def my_half(array):
        return lax.dynamic_slice_in_dim(array, core * HD, HD, 1)

    def send(near, far):
        return near, around(near, 1), around(far, 2)

    mine = my_half(kv_weight)
    others = my_half(other_weight)
    pair_blocks = 2 * rows // BLK
    spare = (pair_blocks - (MAXDOC - 1) % pair_blocks) * BLK
    if slots == 4:

        def multiply(*sets):
            return project(own_tokens, other_tokens, sets, spare)

        slab = jnp.concatenate([mine, others], axis=0)
        token = slab[:16, :]
        x0 = over_dp(slab, 1)
        y0 = over_dp(slab, 2)
        z1 = around(slab, 1)
        token = pause(token, x0, y0, other_tokens, other_queries)
        z3 = around(after(slab, token), 3)
        d0 = over_dp(after(x0, token), 2)
        token = pause(token, z1)
        x1 = over_dp(after(z1, token), 1)
        y1 = over_dp(after(z1, token), 2)
        z2 = around(after(slab, token), 2)
        token = pause(token, z3, d0)
        x3 = over_dp(after(z3, token), 1)
        y3 = over_dp(after(z3, token), 2)
        token = pause(token, x1, y1, z2)
        x2 = over_dp(after(z2, token), 1)
        y2 = over_dp(after(z2, token), 2)
        token = pause(token, x3, y3)
        own_kv = multiply([after(slab, token), z1, z2, z3])
        own_kv = send(*own_kv)
        token = pause(token, own_kv[0], x2, y2)
        d1 = over_dp(after(y1, token), 1)
        d3 = over_dp(after(x3, token), 2)
        d2 = over_dp(after(y2, token), 1)
        xy_near, xy_far = multiply([x0, x1, after(x2, token), x3], [y0, y1, y2, y3])
        token = pause(token, xy_near, own_kv[1], own_kv[2])
        xy_kv = send(after(xy_near, token), after(xy_far, token))
        token = pause(token, d1, d2, d3)
        d_kv = send(*multiply([d0, d1, after(d2, token), d3]))
        token = pause(token, d_kv[0])
    else:
        even = jnp.where(core == 0, mine, others)
        odd = jnp.where(core == 0, others, mine)
        groups = [list(range(0, size, 2)), list(range(1, size, 2))]
        slab = jnp.concatenate([even, odd], axis=0)
        own_set = lax.all_gather(slab, "ctx", axis=0, axis_index_groups=groups, tiled=True)
        pair_tokens = jnp.where(
            core == 0,
            jnp.concatenate([own_tokens, other_tokens], axis=0),
            jnp.concatenate([other_tokens, own_tokens], axis=0),
        )

        def multiply(*sets):
            parts = [
                jnp.dot(pair_tokens, w, preferred_element_type=jnp.float32).astype(jnp.bfloat16)
                for w in sets
            ]
            return jnp.concatenate(parts, axis=0), jnp.concatenate(
                [part[spare:] for part in parts], axis=0
            )

        x_set = over_dp(own_set, 1)
        y_set = over_dp(own_set, 2)
        d_set = over_dp(x_set, 2)
        own_kv = send(*multiply(own_set))
        xy_kv = send(*multiply(x_set, y_set))
        d_kv = send(*multiply(d_set))
        token = slab[:16, :]

    def attend_with(second, one, other):
        return attend(
            second, doc_blocks, block_mask, plan, own_queries, other_queries, one, other
        )

    own_near, own_back, own_far = own_kv
    first = attend_with(0, (0, after(own_near, token), own_back, own_far), (1,) + xy_kv)
    second = attend_with(1, (0,) + xy_kv, (0,) + d_kv)
    got_a, got_b = other_core(first[1]), other_core(second[1])
    st_got_a, st_got_b = other_core(first[3]), other_core(second[3])
    vmem = pl.BlockSpec(memory_space=pltpu.VMEM)
    return pl.pallas_call(
        finish_kernel,
        out_shape=(
            jax.ShapeDtypeStruct((1, rows, QH * HD), jnp.bfloat16),
            jax.ShapeDtypeStruct((1, QH, rows), jnp.float32),
        ),
        in_specs=[vmem] * 8,
        out_specs=(vmem, vmem),
        compiler_params=pltpu.CompilerParams(vmem_limit_bytes=VMEM_LIMIT),
    )(first[0], second[0], got_a, got_b, first[2], second[2], st_got_a, st_got_b)


def solution(mesh):
    in_specs = (
        P("dp", "ctx", None),
        P("dp", "ctx", None),
        P("ctx", "dp"),
        P("dp", None),
        P("dp", None, None),
        P("dp", None),
    )
    out_specs = (P("dp", "ctx", None), P("dp", None, "ctx"))
    return jax.shard_map(body, mesh=mesh, in_specs=in_specs, out_specs=out_specs, check_vma=False)
```

```python
import functools
import math

import jax
import jax.numpy as jnp
from jax import lax
from jax.experimental import pallas as pl
from jax.experimental.pallas import tpu as pltpu
from jax.sharding import PartitionSpec as P

HD = 128
QH = 16
KVH = 4
BLK = 128
MAXDOC = 8
GROUP = QH // KVH
LANES = GROUP * BLK
VMEM_LIMIT = 20 * 1024 * 1024
SCALE = 1.0 / math.sqrt(HD)
LOG2E = 1.0 / math.log(2.0)


def over_dp(array, mask):
    return lax.ppermute(array, "dp", [(i, i ^ mask) for i in range(lax.axis_size("dp"))])


def other_core(array):
    return lax.ppermute(array, "ctx", [(i, i ^ 1) for i in range(lax.axis_size("ctx"))])


def around(array, pairs):
    size = lax.axis_size("ctx")
    return lax.ppermute(array, "ctx", [(i, (i + 2 * pairs) % size) for i in range(size)])


def tie(*arrays):
    return lax.optimization_barrier(arrays)


def project_kernel(slots, steps, sets, passed, has_sum, last, keep, depth, *refs):
    refs = list(refs)
    whole = keep is not None
    tokens = [refs.pop(0) for _ in range(2 if whole else 1)]
    weights = []
    for _ in range(len(steps) * sets):
        array = refs.pop(0)
        if array.shape[0] == depth:
            weights.append(((array, 0), (refs.pop(0), 0)))
        else:
            weights.append(((array, 0), (array, depth)))
    kept_ref = refs.pop() if keep else None
    out_ref = refs.pop()
    extras = refs
    device = lax.axis_index("ctx")
    core, pair = device % 2, device // 2
    rows = tokens[0].shape[0] // (1 if whole else 2)

    def group_columns(step, half):
        source = lax.rem(pair + slots - step, slots)
        group = 2 * source + (core + half) % 2
        return pl.ds(pl.multiple_of(group * depth, depth), depth)

    for side in range(2):
        place = core if side == 0 else 1 - core
        here = pl.ds(pl.multiple_of(place * rows, rows), rows)
        if has_sum:
            total = extras[0][here, :]
        else:
            total = jnp.zeros((rows, sets * HD), jnp.float32)
        for position, step in enumerate(steps):
            for half in range(2):
                if whole:
                    piece = tokens[side][:, group_columns(step, half)]
                else:
                    at = (2 * (step - steps[0]) + half) * depth
                    piece = tokens[0][side * rows : (side + 1) * rows, at : at + depth]
                parts = [weights[s * len(steps) + position][half] for s in range(sets)]
                weight = jnp.concatenate([array[at : at + depth, :] for array, at in parts], axis=1)
                total += jnp.dot(piece, weight, preferred_element_type=jnp.float32)
        for position, step in enumerate(keep or ()):
            for half in range(2):
                at = (2 * position + half) * depth
                kept_ref[side * rows : (side + 1) * rows, at : at + depth] = tokens[side][
                    :, group_columns(step, half)
                ]
        if not last:
            out_ref[here, :] = total
            continue
        total = total.astype(jnp.bfloat16)
        for s in range(sets):
            at = pl.multiple_of(s * 2 * rows + place * rows, rows)
            out_ref[pl.ds(at, rows), :] = total[:, s * HD : (s + 1) * HD]
    at = sets * 2 * rows
    for begin, end in passed:
        out_ref[at : at + end - begin, :] = extras[-1][begin:end, :]
        at += end - begin


def project(tokens, slots, steps, sets, total=None, last=True, passed=(), extra=None, keep=()):
    whole = len(tokens) == 2
    rows = tokens[0].shape[0] * len(tokens)
    weights = []
    for one in sets:
        for w in one:
            weights += w if isinstance(w, tuple) else [w]
    first = sets[0][0]
    depth = first[0].shape[0] if isinstance(first, tuple) else first.shape[0] // 2
    extras = [array for array in (total, extra) if array is not None]
    count = len(sets)
    tall = count * rows + sum(end - begin for begin, end in passed)
    if last:
        out = [jax.ShapeDtypeStruct((tall, HD), jnp.bfloat16)]
    else:
        out = [jax.ShapeDtypeStruct((rows, count * HD), jnp.float32)]
    if keep:
        out.append(jax.ShapeDtypeStruct((rows, len(keep) * 2 * depth), jnp.bfloat16))
    spec = pl.BlockSpec(memory_space=pltpu.VMEM)
    got = pl.pallas_call(
        functools.partial(
            project_kernel,
            slots,
            steps,
            count,
            passed,
            total is not None,
            last,
            keep if whole else None,
            depth,
        ),
        out_shape=tuple(out),
        in_specs=[spec] * (len(tokens) + len(weights) + len(extras)),
        out_specs=(spec,) * len(out),
        compiler_params=pltpu.CompilerParams(vmem_limit_bytes=VMEM_LIMIT),
        cost_estimate=pl.CostEstimate(
            flops=4 * rows * depth * HD * len(steps) * count,
            bytes_accessed=4 * rows * depth * len(steps),
            transcendentals=0,
        ),
    )(*tokens, *weights, *extras)
    return got if keep else got[0]


def document_start(docs_ref, block):
    def ends(j, carry):
        end, start = carry
        end = end + docs_ref[0, j]
        return end, jnp.where(end <= block, end, start)

    return lax.fori_loop(0, docs_ref.shape[1], ends, (jnp.int32(0), jnp.int32(0)))[1]


def score_blocks(keys, query, steps, found, causal, table):
    got = lax.dot_general(
        jnp.concatenate([keys(step) for step in steps], axis=0),
        query,
        (((1,), (1,)), ((), ())),
        preferred_element_type=jnp.float32,
    )
    best = None
    for at, step in enumerate(steps):
        part = got[at * BLK : (at + 1) * BLK, :]
        keep = causal if step == 0 and causal is not None else step < found
        part = jnp.where(keep, part, -jnp.inf)
        table[step * BLK : (step + 1) * BLK, :] = part
        best = part if best is None else jnp.maximum(best, part)
    return jnp.max(best, axis=0, keepdims=True)


def weigh_blocks(values, steps, highest, table):
    weights = jnp.exp2(
        (table[steps[0] * BLK : (steps[-1] + 1) * BLK, :] - highest) * (SCALE * LOG2E)
    )
    part = lax.dot_general(
        jnp.concatenate([values(step) for step in steps], axis=0),
        weights.astype(jnp.bfloat16),
        (((0,), (0,)), ((), ())),
        preferred_element_type=jnp.float32,
    )
    return jnp.sum(weights, axis=0, keepdims=True), part


def where_am_i(second):
    device = lax.axis_index("ctx")
    slice_of = lax.axis_index("dp")
    core, pair = device % 2, device // 2
    column, kind = slice_of % 2, slice_of // 2
    return core, pair, kind, 2 * ((column + second) % 2) + core


def stack_kernel(docs_ref, mask_ref, plan_ref, q_own_ref, q_other_ref, out_ref, facts):
    core, pair, _, _ = where_am_i(0)
    blocks = q_own_ref.shape[0] // BLK
    for side in range(2):
        for place in range(blocks):
            item = side * blocks + place
            index = (core if side == 0 else 1 - core) * blocks + place
            block = 2 * blocks * pair + index
            start = document_start(docs_ref, block)
            for back in range(1, MAXDOC):
                admitted = jnp.logical_and(
                    block - back >= start, mask_ref[0, block, back - 1] == 1
                )
                facts[item, back] = admitted.astype(jnp.int32)
            facts[item, 0] = index
            facts[item, MAXDOC] = plan_ref[0, block] - 2 * blocks * pair
    for second in range(2):
        head = where_am_i(second)[3]
        columns = pl.ds(pl.multiple_of(head * LANES, LANES), LANES)
        for side, q_ref in enumerate((q_own_ref, q_other_ref)):
            for place in range(blocks):
                query = q_ref[place * BLK : (place + 1) * BLK, columns]
                for g in range(GROUP):
                    out_ref[second, side * blocks + place, g * BLK : (g + 1) * BLK, :] = query[
                        :, g * HD : (g + 1) * HD
                    ]


def stack(docs, mask, plan, q_own, q_other):
    vmem = pl.BlockSpec(memory_space=pltpu.VMEM)
    smem = pl.BlockSpec(memory_space=pltpu.SMEM)
    items = 2 * q_own.shape[0] // BLK
    return pl.pallas_call(
        stack_kernel,
        out_shape=(
            jax.ShapeDtypeStruct((2, items, LANES, HD), jnp.bfloat16),
            jax.ShapeDtypeStruct((items, MAXDOC + 1), jnp.int32),
        ),
        in_specs=[smem] * 3 + [vmem] * 2,
        out_specs=(vmem, smem),
        compiler_params=pltpu.CompilerParams(vmem_limit_bytes=VMEM_LIMIT),
        cost_estimate=pl.CostEstimate(
            flops=0, bytes_accessed=4 * items * LANES * HD, transcendentals=0
        ),
    )(docs, mask, plan, q_own, q_other)


def near_kernel(
    second,
    starts,
    facts,
    queries_ref,
    near_a,
    near_b,
    back_a,
    back_b,
    summed,
    stat,
    kv,
    table,
    places,
):
    kind = where_am_i(second)[2]
    pair_blocks = queries_ref.shape[1]
    tall = pair_blocks * BLK
    for which, near, back, at in (
        (kind, near_a, back_a, starts[0]),
        (1 - kind, near_b, back_b, starts[1]),
    ):
        kv[which, :tall, :] = back[at[1] : at[1] + tall, :]
        kv[which, tall:, :] = near[at[0] : at[0] + tall, :]
    causal = lax.broadcasted_iota(jnp.int32, (BLK, BLK), 0) <= lax.broadcasted_iota(
        jnp.int32, (BLK, BLK), 1
    )
    causal = jnp.tile(causal, (1, GROUP))

    for item in range(pair_blocks):
        index = facts[item, 0]
        for step in range(MAXDOC + 1):
            places[step] = tall + index * BLK
        found = jnp.int32(1)
        for back in range(1, MAXDOC):
            places[found] = tall + (index - back) * BLK
            found += jnp.where(back <= index + pair_blocks, facts[item, back], 0)
        places[found] = tall + index * BLK
        rows = queries_ref[second, item]

        def fetch(which, step):
            return kv[which, pl.ds(pl.multiple_of(places[step], BLK), BLK), :]

        keys = functools.partial(fetch, 0)
        values = functools.partial(fetch, 1)
        half = MAXDOC // 2
        low, high = range(half), range(half, MAXDOC)
        stat[item, 0:1, :] = score_blocks(keys, rows, low, found, causal, table)

        @pl.when(found > half)
        def _():
            stat[item, 0:1, :] = jnp.maximum(
                stat[item, 0:1, :], score_blocks(keys, rows, high, found, None, table)
            )

        stat[item, 1:2, :], summed[item] = weigh_blocks(values, low, stat[item, 0:1, :], table)

        @pl.when(found > half)
        def _():
            more, part = weigh_blocks(values, high, stat[item, 0:1, :], table)
            stat[item, 1:2, :] += more
            summed[item] += part


def far_kernel(
    second,
    starts,
    facts,
    summed_ref,
    stat_ref,
    queries_ref,
    far_a,
    far_b,
    out_own,
    out_other,
    stats_own,
    stats_other,
    kv,
    table,
    top,
    total,
    summed,
    places,
):
    core, _, kind, _ = where_am_i(second)
    pair_blocks = queries_ref.shape[1]
    dev_blocks = pair_blocks // 2
    far_blocks = (MAXDOC - 1) % pair_blocks
    short = far_blocks * BLK
    for which, far, at in ((kind, far_a, starts[0]), (1 - kind, far_b, starts[1])):
        kv[which, :, :] = far[at[2] : at[2] + short, :]

    for item in range(pair_blocks):
        side, place = divmod(item, dev_blocks)
        out_ref = (out_own, out_other)[side]
        rows = slice(place * BLK, (place + 1) * BLK)
        index = facts[item, 0]
        for step in range(far_blocks + 1):
            places[step] = 0
        found = jnp.int32(0)
        for back in range(MAXDOC - far_blocks, MAXDOC):
            places[found] = (far_blocks + pair_blocks + index - back) * BLK
            found += jnp.where(back > index + pair_blocks, facts[item, back], 0)
        places[found] = 0
        top[...] = stat_ref[item, 0:1, :]
        total[...] = stat_ref[item, 1:2, :]
        summed[...] = summed_ref[item]

        @pl.when(found > 0)
        def _():
            query = queries_ref[second, item]

            def fetch(which, step):
                return kv[which, pl.ds(pl.multiple_of(places[step], BLK), BLK), :]

            steps = range(far_blocks)
            before = top[...]
            highest = jnp.maximum(
                before,
                score_blocks(functools.partial(fetch, 0), query, steps, found, None, table),
            )
            more, part = weigh_blocks(functools.partial(fetch, 1), steps, highest, table)
            shrink = jnp.exp2((before - highest) * (SCALE * LOG2E))
            top[...] = highest
            total[...] = total[...] * shrink + more
            summed[...] = summed[...] * shrink + part

        result = summed[...] / total[...]
        for g in range(GROUP):
            out_ref[rows, g * HD : (g + 1) * HD] = (
                result[:, g * BLK : (g + 1) * BLK].T.astype(jnp.bfloat16)
            )
        lse = top[...] * SCALE + jnp.log(total[...])
        slot = facts[item, MAXDOC]
        keep_here = slot // dev_blocks == core
        slot_at = slot % dev_blocks

        @pl.when(keep_here)
        def _():
            for g in range(GROUP):
                stats_own[slot_at, g : g + 1, :] = lse[:, g * BLK : (g + 1) * BLK]

        @pl.when(jnp.logical_not(keep_here))
        def _():
            for g in range(GROUP):
                stats_other[slot_at, g : g + 1, :] = lse[:, g * BLK : (g + 1) * BLK]


def attend_near(second, facts, queries, first_set, second_set):
    vmem = pl.BlockSpec(memory_space=pltpu.VMEM)
    smem = pl.BlockSpec(memory_space=pltpu.SMEM)
    items = queries.shape[1]
    (near_a, back_a, _), start_a = first_set
    (near_b, back_b, _), start_b = second_set
    return pl.pallas_call(
        functools.partial(near_kernel, second, (start_a, start_b)),
        out_shape=(
            jax.ShapeDtypeStruct((items, HD, LANES), jnp.float32),
            jax.ShapeDtypeStruct((items, 8, LANES), jnp.float32),
        ),
        in_specs=[smem] + [vmem] * 5,
        out_specs=(vmem,) * 2,
        scratch_shapes=[
            pltpu.VMEM((2, 2 * items * BLK, HD), jnp.bfloat16),
            pltpu.VMEM((MAXDOC * BLK, LANES), jnp.float32),
            pltpu.SMEM((MAXDOC + 1,), jnp.int32),
        ],
        compiler_params=pltpu.CompilerParams(vmem_limit_bytes=VMEM_LIMIT),
        cost_estimate=pl.CostEstimate(
            flops=items * MAXDOC * BLK * LANES * HD * 4,
            bytes_accessed=4 * items * BLK * QH * HD,
            transcendentals=items * MAXDOC * BLK * LANES,
        ),
    )(facts, queries, near_a, near_b, back_a, back_b)


def attend_far(second, facts, queries, carried, first_set, second_set):
    vmem = pl.BlockSpec(memory_space=pltpu.VMEM)
    smem = pl.BlockSpec(memory_space=pltpu.SMEM)
    items = queries.shape[1]
    dev_blocks = items // 2
    rows = dev_blocks * BLK
    far_blocks = (MAXDOC - 1) % items
    (_, _, far_a), start_a = first_set
    (_, _, far_b), start_b = second_set
    out = jax.ShapeDtypeStruct((rows, LANES), jnp.bfloat16)
    stats = jax.ShapeDtypeStruct((dev_blocks, GROUP, BLK), jnp.float32)
    return pl.pallas_call(
        functools.partial(far_kernel, second, (start_a, start_b)),
        out_shape=(out, out, stats, stats),
        in_specs=[smem] + [vmem] * 5,
        out_specs=(vmem,) * 4,
        scratch_shapes=[
            pltpu.VMEM((2, far_blocks * BLK, HD), jnp.bfloat16),
            pltpu.VMEM((far_blocks * BLK, LANES), jnp.float32),
            pltpu.VMEM((1, LANES), jnp.float32),
            pltpu.VMEM((1, LANES), jnp.float32),
            pltpu.VMEM((HD, LANES), jnp.float32),
            pltpu.SMEM((far_blocks + 1,), jnp.int32),
        ],
        compiler_params=pltpu.CompilerParams(vmem_limit_bytes=VMEM_LIMIT),
        cost_estimate=pl.CostEstimate(
            flops=items * far_blocks * BLK * LANES * HD * 4,
            bytes_accessed=8 * rows * LANES,
            transcendentals=items * far_blocks * BLK * LANES,
        ),
    )(facts, *carried, queries, far_a, far_b)


def finish_kernel(
    own_a, own_b, got_a, got_b, st_own_a, st_own_b, st_got_a, st_got_b, out_ref, stats_ref
):
    core = lax.axis_index("ctx") % 2
    column = lax.axis_index("dp") % 2
    pieces = (
        (own_a, column, core),
        (own_b, 1 - column, core),
        (got_a, column, 1 - core),
        (got_b, 1 - column, 1 - core),
    )
    for piece, head_pair, side in pieces:
        head = 2 * head_pair + side
        out_ref[0, :, pl.ds(pl.multiple_of(head * LANES, LANES), LANES)] = piece[...]
    for head in range(KVH):
        is_a = head // 2 == column
        is_own = head % 2 == core
        own = jnp.where(is_a, st_own_a[...], st_own_b[...])
        got = jnp.where(is_a, st_got_a[...], st_got_b[...])
        lse = jnp.where(is_own, own, got)
        for place in range(lse.shape[0]):
            stats_ref[0, head * GROUP : (head + 1) * GROUP, place * BLK : (place + 1) * BLK] = lse[place]


def body(tokens, queries, kv_weight, doc_blocks, block_mask, plan):
    size = lax.axis_size("ctx")
    device = lax.axis_index("ctx")
    core = device % 2
    slots = size // 2
    own_tokens, own_queries = tokens[0], queries[0]
    rows = own_tokens.shape[0]
    other_weight = other_core(kv_weight)
    other_weight, own_tokens, own_queries = tie(other_weight, own_tokens, own_queries)
    other_queries = other_core(own_queries)

    def my_half(array):
        return lax.dynamic_slice_in_dim(array, core * HD, HD, 1)

    other_tokens = other_core(own_tokens)
    mine = my_half(kv_weight)
    others = my_half(other_weight)
    tall = 2 * rows
    spare = tall - (MAXDOC - 1) % (tall // BLK) * BLK
    short = tall - spare
    step_xy = ((spare, tall),)
    step_d = ((spare, tall), (tall + spare, 2 * tall))
    if slots == 4:

        def multiply(steps, sets, *rest, **more):
            return project((own_tokens, other_tokens), slots, steps, sets, *rest, **more)

        def multiply_kept(steps, sets, *rest, **more):
            return project((kept,), slots, steps, sets, *rest, **more)

        slab = jnp.concatenate([mine, others], axis=0)
        x0 = over_dp(slab, 1)
        y0 = over_dp(slab, 2)
        z1 = around(slab, 1)
        stacked, facts = stack(doc_blocks, block_mask, plan, own_queries, other_queries)
        slab, x0, y0, other_tokens, stacked, facts = tie(
            slab, x0, y0, other_tokens, stacked, facts
        )
        z3 = around(slab, 3)
        d0 = over_dp(x0, 2)
        slab, z1 = tie(slab, z1)
        z2 = around(slab, 2)
        x1 = over_dp(z1, 1)
        y1 = over_dp(z1, 2)
        z3, d0 = tie(z3, d0)
        x3 = over_dp(z3, 1)
        y3 = over_dp(z3, 2)
        half = slab.shape[0] // 2

        def diagonal(x, y):
            return over_dp(x[:half], 2), over_dp(y[half:], 1)

        d1_low, d1_high = diagonal(x1, y1)
        z2, d1_low, d1_high = tie(z2, d1_low, d1_high)
        x2 = over_dp(z2, 1)
        y2 = over_dp(z2, 2)
        slab, z1, z2, z3, x1, y1 = tie(slab, z1, z2, z3, x1, y1)
        own_near, kept = multiply((0, 1, 2, 3), [[slab, z1, z2, z3]], keep=(2, 3))
        own_back = around(own_near, 1)
        own_near, x3, y3 = tie(own_near, x3, y3)
        xy_sum = multiply((0, 1, 3), [[x0, x1, x3], [y0, y1, y3]], last=False)
        xy_sum, x2, y2, x3, y3 = tie(xy_sum, x2, y2, x3, y3)
        d2 = diagonal(x2, y2)
        d3 = diagonal(x3, y3)
        xy_near = multiply_kept((2,), [[x2], [y2]], xy_sum, passed=step_xy, extra=own_back)
        xy_back = around(xy_near, 1)
        d0, d1_low, d1_high, xy_near = tie(d0, d1_low, d1_high, xy_near)
        d1 = (d1_low, d1_high)
        d_sum = multiply((0, 1), [[d0, d1]], last=False)
        d_near = multiply_kept((2, 3), [[d2, d3]], d_sum, passed=step_d, extra=xy_back)
        d_back = around(d_near, 1)
        d_far = around(d_back[spare:tall], 1)
    else:
        stacked, facts = stack(doc_blocks, block_mask, plan, own_queries, other_queries)
        even = jnp.where(core == 0, mine, others)
        odd = jnp.where(core == 0, others, mine)
        groups = [list(range(0, size, 2)), list(range(1, size, 2))]
        slab = jnp.concatenate([even, odd], axis=0)
        own_set = lax.all_gather(slab, "ctx", axis=0, axis_index_groups=groups, tiled=True)
        pair_tokens = jnp.where(
            core == 0,
            jnp.concatenate([own_tokens, other_tokens], axis=0),
            jnp.concatenate([other_tokens, own_tokens], axis=0),
        )

        def multiply(sets, passed=(), extra=None):
            parts = [
                jnp.dot(pair_tokens, w, preferred_element_type=jnp.float32).astype(jnp.bfloat16)
                for w in sets
            ]
            parts += [extra[begin:end] for begin, end in passed]
            return jnp.concatenate(parts, axis=0)

        x_set = over_dp(own_set, 1)
        y_set = over_dp(own_set, 2)
        d_set = over_dp(x_set, 2)
        own_near = multiply([own_set])
        own_back = around(own_near, 1)
        xy_near = multiply([x_set, y_set], step_xy, own_back)
        xy_back = around(xy_near, 1)
        d_near = multiply([d_set], step_d, xy_back)
        d_back = around(d_near, 1)
        d_far = around(d_back[spare:tall], 1)

    own_set = (own_near, own_back, xy_back), (0, 0, 2 * tall)
    y_set = (xy_near, xy_back, d_back), (tall, tall, tall + short)
    x_set = (xy_near, xy_back, d_back), (0, 0, tall)
    d_set = (d_near, d_back, d_far), (0, 0, 0)
    near_a = attend_near(0, facts, stacked, own_set, y_set)
    near_b = attend_near(1, facts, stacked, x_set, d_set)
    first = attend_far(0, facts, stacked, near_a, own_set, y_set)
    second = attend_far(1, facts, stacked, near_b, x_set, d_set)
    got_a, got_b = other_core(first[1]), other_core(second[1])
    st_got_a, st_got_b = other_core(first[3]), other_core(second[3])
    vmem = pl.BlockSpec(memory_space=pltpu.VMEM)
    return pl.pallas_call(
        finish_kernel,
        out_shape=(
            jax.ShapeDtypeStruct((1, rows, QH * HD), jnp.bfloat16),
            jax.ShapeDtypeStruct((1, QH, rows), jnp.float32),
        ),
        in_specs=[vmem] * 8,
        out_specs=(vmem, vmem),
        compiler_params=pltpu.CompilerParams(vmem_limit_bytes=VMEM_LIMIT),
    )(first[0], second[0], got_a, got_b, first[2], second[2], st_got_a, st_got_b)


def solution(mesh):
    in_specs = (
        P("dp", "ctx", None),
        P("dp", "ctx", None),
        P("ctx", "dp"),
        P("dp", None),
        P("dp", None, None),
        P("dp", None),
    )
    out_specs = (P("dp", "ctx", None), P("dp", None, "ctx"))
    return jax.shard_map(body, mesh=mesh, in_specs=in_specs, out_specs=out_specs, check_vma=False)
```

```python
import functools
import math

import jax
import jax.numpy as jnp
from jax import lax
from jax.experimental import pallas as pl
from jax.experimental.pallas import tpu as pltpu
from jax.sharding import PartitionSpec as P

HD = 128
QH = 16
KVH = 4
BLK = 128
MAXDOC = 8
GROUP = QH // KVH
LANES = GROUP * BLK
VMEM_LIMIT = 20 * 1024 * 1024
SCALE = 1.0 / math.sqrt(HD)
LOG2E = 1.0 / math.log(2.0)


def over_dp(array, mask):
    return lax.ppermute(array, "dp", [(i, i ^ mask) for i in range(lax.axis_size("dp"))])


def other_core(array):
    return lax.ppermute(array, "ctx", [(i, i ^ 1) for i in range(lax.axis_size("ctx"))])


def around(array, pairs):
    size = lax.axis_size("ctx")
    return lax.ppermute(array, "ctx", [(i, (i + 2 * pairs) % size) for i in range(size)])


def neighbours(array):
    return lax.ppermute(array, "ctx", [(i, i ^ 2) for i in range(lax.axis_size("ctx"))])


def mirrored(array):
    size = lax.axis_size("ctx")
    pairs = [(i, size - 2 - 2 * (i // 2) + i % 2) for i in range(size)]
    return lax.ppermute(array, "ctx", pairs)


def tie(*arrays):
    return lax.optimization_barrier(arrays)


def project_kernel(steps, sets, passed, has_sum, last, keep, depth, *refs):
    refs = list(refs)
    whole = keep is not None
    tokens = [refs.pop(0) for _ in range(2 if whole else 1)]
    weights = []
    for _ in range(len(steps) * sets):
        array = refs.pop(0)
        if array.shape[0] == depth:
            weights.append(((array, 0), (refs.pop(0), 0)))
        else:
            weights.append(((array, 0), (array, depth)))
    kept_ref = refs.pop() if keep else None
    out_ref = refs.pop()
    extras = refs
    device = lax.axis_index("ctx")
    core, pair = device % 2, device // 2
    rows = tokens[0].shape[0] // (1 if whole else 2)

    sources = (pair, pair + 1 - 2 * lax.rem(pair, 2), lax.rem(pair + 2, 4), 3 - pair)

    def group_columns(step, half):
        source = sources[step]
        group = 2 * source + (core + half) % 2
        return pl.ds(pl.multiple_of(group * depth, depth), depth)

    for side in range(2):
        place = core if side == 0 else 1 - core
        here = pl.ds(pl.multiple_of(place * rows, rows), rows)
        if has_sum:
            total = extras[0][here, :]
        else:
            total = jnp.zeros((rows, sets * HD), jnp.float32)
        for position, step in enumerate(steps):
            for half in range(2):
                if whole:
                    piece = tokens[side][:, group_columns(step, half)]
                else:
                    at = (2 * (step - steps[0]) + half) * depth
                    piece = tokens[0][side * rows : (side + 1) * rows, at : at + depth]
                parts = [weights[s * len(steps) + position][half] for s in range(sets)]
                weight = jnp.concatenate([array[at : at + depth, :] for array, at in parts], axis=1)
                total += jnp.dot(piece, weight, preferred_element_type=jnp.float32)
        for position, step in enumerate(keep or ()):
            for half in range(2):
                at = (2 * position + half) * depth
                kept_ref[side * rows : (side + 1) * rows, at : at + depth] = tokens[side][
                    :, group_columns(step, half)
                ]
        if not last:
            out_ref[here, :] = total
            continue
        total = total.astype(jnp.bfloat16)
        for s in range(sets):
            at = pl.multiple_of(s * 2 * rows + place * rows, rows)
            out_ref[pl.ds(at, rows), :] = total[:, s * HD : (s + 1) * HD]
    at = sets * 2 * rows
    for begin, end in passed:
        out_ref[at : at + end - begin, :] = extras[-1][begin:end, :]
        at += end - begin


def project(tokens, steps, sets, total=None, last=True, passed=(), extra=None, keep=()):
    whole = len(tokens) == 2
    rows = tokens[0].shape[0] * len(tokens)
    weights = []
    for one in sets:
        for w in one:
            weights += w if isinstance(w, tuple) else [w]
    first = sets[0][0]
    depth = first[0].shape[0] if isinstance(first, tuple) else first.shape[0] // 2
    extras = [array for array in (total, extra) if array is not None]
    count = len(sets)
    tall = count * rows + sum(end - begin for begin, end in passed)
    if last:
        out = [jax.ShapeDtypeStruct((tall, HD), jnp.bfloat16)]
    else:
        out = [jax.ShapeDtypeStruct((rows, count * HD), jnp.float32)]
    if keep:
        out.append(jax.ShapeDtypeStruct((rows, len(keep) * 2 * depth), jnp.bfloat16))
    spec = pl.BlockSpec(memory_space=pltpu.VMEM)
    got = pl.pallas_call(
        functools.partial(
            project_kernel,
            steps,
            count,
            passed,
            total is not None,
            last,
            keep if whole else None,
            depth,
        ),
        out_shape=tuple(out),
        in_specs=[spec] * (len(tokens) + len(weights) + len(extras)),
        out_specs=(spec,) * len(out),
        compiler_params=pltpu.CompilerParams(vmem_limit_bytes=VMEM_LIMIT),
        cost_estimate=pl.CostEstimate(
            flops=4 * rows * depth * HD * len(steps) * count,
            bytes_accessed=4 * rows * depth * len(steps),
            transcendentals=0,
        ),
    )(*tokens, *weights, *extras)
    return got if keep else got[0]


def document_start(docs_ref, block):
    def ends(j, carry):
        end, start = carry
        end = end + docs_ref[0, j]
        return end, jnp.where(end <= block, end, start)

    return lax.fori_loop(0, docs_ref.shape[1], ends, (jnp.int32(0), jnp.int32(0)))[1]


def score_blocks(keys, query, steps, found, causal, table):
    got = lax.dot_general(
        jnp.concatenate([keys(step) for step in steps], axis=0),
        query,
        (((1,), (1,)), ((), ())),
        preferred_element_type=jnp.float32,
    )
    best = None
    for at, step in enumerate(steps):
        part = got[at * BLK : (at + 1) * BLK, :]
        keep = causal if step == 0 and causal is not None else step < found
        part = jnp.where(keep, part, -jnp.inf)
        table[step * BLK : (step + 1) * BLK, :] = part
        best = part if best is None else jnp.maximum(best, part)
    return jnp.max(best, axis=0, keepdims=True)


def weigh_blocks(values, steps, highest, table):
    weights = jnp.exp2(
        (table[steps[0] * BLK : (steps[-1] + 1) * BLK, :] - highest) * (SCALE * LOG2E)
    )
    part = lax.dot_general(
        jnp.concatenate([values(step) for step in steps], axis=0),
        weights.astype(jnp.bfloat16),
        (((0,), (0,)), ((), ())),
        preferred_element_type=jnp.float32,
    )
    return jnp.sum(weights, axis=0, keepdims=True), part


def where_am_i(second):
    device = lax.axis_index("ctx")
    slice_of = lax.axis_index("dp")
    core, pair = device % 2, device // 2
    column, kind = slice_of % 2, slice_of // 2
    return core, pair, kind, 2 * ((column + second) % 2) + core


def stack_kernel(docs_ref, mask_ref, plan_ref, q_own_ref, q_other_ref, out_ref, facts):
    core, pair, _, _ = where_am_i(0)
    blocks = q_own_ref.shape[0] // BLK
    for side in range(2):
        for place in range(blocks):
            item = side * blocks + place
            index = (core if side == 0 else 1 - core) * blocks + place
            block = 2 * blocks * pair + index
            start = document_start(docs_ref, block)
            for back in range(1, MAXDOC):
                admitted = jnp.logical_and(
                    block - back >= start, mask_ref[0, block, back - 1] == 1
                )
                facts[item, back] = admitted.astype(jnp.int32)
            facts[item, 0] = index
            facts[item, MAXDOC] = plan_ref[0, block] - 2 * blocks * pair
    for second in range(2):
        head = where_am_i(second)[3]
        columns = pl.ds(pl.multiple_of(head * LANES, LANES), LANES)
        for side, q_ref in enumerate((q_own_ref, q_other_ref)):
            for place in range(blocks):
                query = q_ref[place * BLK : (place + 1) * BLK, columns]
                for g in range(GROUP):
                    out_ref[second, side * blocks + place, g * BLK : (g + 1) * BLK, :] = query[
                        :, g * HD : (g + 1) * HD
                    ]


def stack(docs, mask, plan, q_own, q_other):
    vmem = pl.BlockSpec(memory_space=pltpu.VMEM)
    smem = pl.BlockSpec(memory_space=pltpu.SMEM)
    items = 2 * q_own.shape[0] // BLK
    return pl.pallas_call(
        stack_kernel,
        out_shape=(
            jax.ShapeDtypeStruct((2, items, LANES, HD), jnp.bfloat16),
            jax.ShapeDtypeStruct((items, MAXDOC + 1), jnp.int32),
        ),
        in_specs=[smem] * 3 + [vmem] * 2,
        out_specs=(vmem, smem),
        compiler_params=pltpu.CompilerParams(vmem_limit_bytes=VMEM_LIMIT),
        cost_estimate=pl.CostEstimate(
            flops=0, bytes_accessed=4 * items * LANES * HD, transcendentals=0
        ),
    )(docs, mask, plan, q_own, q_other)


def near_kernel(
    second,
    starts,
    facts,
    queries_ref,
    near_a,
    near_b,
    back_a,
    back_b,
    summed,
    stat,
    kv,
    table,
    places,
):
    kind = where_am_i(second)[2]
    pair_blocks = queries_ref.shape[1]
    tall = pair_blocks * BLK
    for which, near, back, at in (
        (kind, near_a, back_a, starts[0]),
        (1 - kind, near_b, back_b, starts[1]),
    ):
        kv[which, :tall, :] = back[at[1] : at[1] + tall, :]
        kv[which, tall:, :] = near[at[0] : at[0] + tall, :]
    causal = lax.broadcasted_iota(jnp.int32, (BLK, BLK), 0) <= lax.broadcasted_iota(
        jnp.int32, (BLK, BLK), 1
    )
    causal = jnp.tile(causal, (1, GROUP))

    for item in range(pair_blocks):
        index = facts[item, 0]
        for step in range(MAXDOC + 1):
            places[step] = tall + index * BLK
        found = jnp.int32(1)
        for back in range(1, MAXDOC):
            places[found] = tall + (index - back) * BLK
            found += jnp.where(back <= index + pair_blocks, facts[item, back], 0)
        places[found] = tall + index * BLK
        rows = queries_ref[second, item]

        def fetch(which, step):
            return kv[which, pl.ds(pl.multiple_of(places[step], BLK), BLK), :]

        keys = functools.partial(fetch, 0)
        values = functools.partial(fetch, 1)
        half = MAXDOC // 2
        low, high = range(half), range(half, MAXDOC)
        stat[item, 0:1, :] = score_blocks(keys, rows, low, found, causal, table)

        @pl.when(found > half)
        def _():
            stat[item, 0:1, :] = jnp.maximum(
                stat[item, 0:1, :], score_blocks(keys, rows, high, found, None, table)
            )

        stat[item, 1:2, :], summed[item] = weigh_blocks(values, low, stat[item, 0:1, :], table)

        @pl.when(found > half)
        def _():
            more, part = weigh_blocks(values, high, stat[item, 0:1, :], table)
            stat[item, 1:2, :] += more
            summed[item] += part


def far_kernel(
    second,
    starts,
    facts,
    summed_ref,
    stat_ref,
    queries_ref,
    far_a,
    far_b,
    out_own,
    out_other,
    stats_own,
    stats_other,
    kv,
    table,
    top,
    total,
    summed,
    places,
):
    core, _, kind, _ = where_am_i(second)
    pair_blocks = queries_ref.shape[1]
    dev_blocks = pair_blocks // 2
    far_blocks = (MAXDOC - 1) % pair_blocks
    short = far_blocks * BLK
    for which, far, at in ((kind, far_a, starts[0]), (1 - kind, far_b, starts[1])):
        kv[which, :, :] = far[at[2] : at[2] + short, :]

    for item in range(pair_blocks):
        side, place = divmod(item, dev_blocks)
        out_ref = (out_own, out_other)[side]
        rows = slice(place * BLK, (place + 1) * BLK)
        index = facts[item, 0]
        for step in range(far_blocks + 1):
            places[step] = 0
        found = jnp.int32(0)
        for back in range(MAXDOC - far_blocks, MAXDOC):
            places[found] = (far_blocks + pair_blocks + index - back) * BLK
            found += jnp.where(back > index + pair_blocks, facts[item, back], 0)
        places[found] = 0
        top[...] = stat_ref[item, 0:1, :]
        total[...] = stat_ref[item, 1:2, :]
        summed[...] = summed_ref[item]

        @pl.when(found > 0)
        def _():
            query = queries_ref[second, item]

            def fetch(which, step):
                return kv[which, pl.ds(pl.multiple_of(places[step], BLK), BLK), :]

            steps = range(far_blocks)
            before = top[...]
            highest = jnp.maximum(
                before,
                score_blocks(functools.partial(fetch, 0), query, steps, found, None, table),
            )
            more, part = weigh_blocks(functools.partial(fetch, 1), steps, highest, table)
            shrink = jnp.exp2((before - highest) * (SCALE * LOG2E))
            top[...] = highest
            total[...] = total[...] * shrink + more
            summed[...] = summed[...] * shrink + part

        result = summed[...] / total[...]
        for g in range(GROUP):
            out_ref[rows, g * HD : (g + 1) * HD] = (
                result[:, g * BLK : (g + 1) * BLK].T.astype(jnp.bfloat16)
            )
        lse = top[...] * SCALE + jnp.log(total[...])
        slot = facts[item, MAXDOC]
        keep_here = slot // dev_blocks == core
        slot_at = slot % dev_blocks

        @pl.when(keep_here)
        def _():
            for g in range(GROUP):
                stats_own[slot_at, g : g + 1, :] = lse[:, g * BLK : (g + 1) * BLK]

        @pl.when(jnp.logical_not(keep_here))
        def _():
            for g in range(GROUP):
                stats_other[slot_at, g : g + 1, :] = lse[:, g * BLK : (g + 1) * BLK]


def attend_near(second, facts, queries, first_set, second_set):
    vmem = pl.BlockSpec(memory_space=pltpu.VMEM)
    smem = pl.BlockSpec(memory_space=pltpu.SMEM)
    items = queries.shape[1]
    (near_a, back_a, _), start_a = first_set
    (near_b, back_b, _), start_b = second_set
    return pl.pallas_call(
        functools.partial(near_kernel, second, (start_a, start_b)),
        out_shape=(
            jax.ShapeDtypeStruct((items, HD, LANES), jnp.float32),
            jax.ShapeDtypeStruct((items, 8, LANES), jnp.float32),
        ),
        in_specs=[smem] + [vmem] * 5,
        out_specs=(vmem,) * 2,
        scratch_shapes=[
            pltpu.VMEM((2, 2 * items * BLK, HD), jnp.bfloat16),
            pltpu.VMEM((MAXDOC * BLK, LANES), jnp.float32),
            pltpu.SMEM((MAXDOC + 1,), jnp.int32),
        ],
        compiler_params=pltpu.CompilerParams(vmem_limit_bytes=VMEM_LIMIT),
        cost_estimate=pl.CostEstimate(
            flops=items * MAXDOC * BLK * LANES * HD * 4,
            bytes_accessed=4 * items * BLK * QH * HD,
            transcendentals=items * MAXDOC * BLK * LANES,
        ),
    )(facts, queries, near_a, near_b, back_a, back_b)


def attend_far(second, facts, queries, carried, first_set, second_set):
    vmem = pl.BlockSpec(memory_space=pltpu.VMEM)
    smem = pl.BlockSpec(memory_space=pltpu.SMEM)
    items = queries.shape[1]
    dev_blocks = items // 2
    rows = dev_blocks * BLK
    far_blocks = (MAXDOC - 1) % items
    (_, _, far_a), start_a = first_set
    (_, _, far_b), start_b = second_set
    out = jax.ShapeDtypeStruct((rows, LANES), jnp.bfloat16)
    stats = jax.ShapeDtypeStruct((dev_blocks, GROUP, BLK), jnp.float32)
    return pl.pallas_call(
        functools.partial(far_kernel, second, (start_a, start_b)),
        out_shape=(out, out, stats, stats),
        in_specs=[smem] + [vmem] * 5,
        out_specs=(vmem,) * 4,
        scratch_shapes=[
            pltpu.VMEM((2, far_blocks * BLK, HD), jnp.bfloat16),
            pltpu.VMEM((far_blocks * BLK, LANES), jnp.float32),
            pltpu.VMEM((1, LANES), jnp.float32),
            pltpu.VMEM((1, LANES), jnp.float32),
            pltpu.VMEM((HD, LANES), jnp.float32),
            pltpu.SMEM((far_blocks + 1,), jnp.int32),
        ],
        compiler_params=pltpu.CompilerParams(vmem_limit_bytes=VMEM_LIMIT),
        cost_estimate=pl.CostEstimate(
            flops=items * far_blocks * BLK * LANES * HD * 4,
            bytes_accessed=8 * rows * LANES,
            transcendentals=items * far_blocks * BLK * LANES,
        ),
    )(facts, *carried, queries, far_a, far_b)


def finish_kernel(
    own_a, own_b, got_a, got_b, st_own_a, st_own_b, st_got_a, st_got_b, out_ref, stats_ref
):
    core = lax.axis_index("ctx") % 2
    column = lax.axis_index("dp") % 2
    pieces = (
        (own_a, column, core),
        (own_b, 1 - column, core),
        (got_a, column, 1 - core),
        (got_b, 1 - column, 1 - core),
    )
    for piece, head_pair, side in pieces:
        head = 2 * head_pair + side
        out_ref[0, :, pl.ds(pl.multiple_of(head * LANES, LANES), LANES)] = piece[...]
    for head in range(KVH):
        is_a = head // 2 == column
        is_own = head % 2 == core
        own = jnp.where(is_a, st_own_a[...], st_own_b[...])
        got = jnp.where(is_a, st_got_a[...], st_got_b[...])
        lse = jnp.where(is_own, own, got)
        for place in range(lse.shape[0]):
            stats_ref[0, head * GROUP : (head + 1) * GROUP, place * BLK : (place + 1) * BLK] = lse[place]


def body(tokens, queries, kv_weight, doc_blocks, block_mask, plan):
    size = lax.axis_size("ctx")
    device = lax.axis_index("ctx")
    core = device % 2
    slots = size // 2
    own_tokens, own_queries = tokens[0], queries[0]
    rows = own_tokens.shape[0]
    other_weight = other_core(kv_weight)
    other_weight, own_tokens, own_queries = tie(other_weight, own_tokens, own_queries)
    other_queries = other_core(own_queries)

    def my_half(array):
        return lax.dynamic_slice_in_dim(array, core * HD, HD, 1)

    other_tokens = other_core(own_tokens)
    mine = my_half(kv_weight)
    others = my_half(other_weight)
    tall = 2 * rows
    spare = tall - (MAXDOC - 1) % (tall // BLK) * BLK
    short = tall - spare
    step_xy = ((spare, tall),)
    step_d = ((spare, tall), (tall + spare, 2 * tall))
    if slots == 4:

        def multiply(steps, sets, *rest, **more):
            return project((own_tokens, other_tokens), steps, sets, *rest, **more)

        def multiply_kept(steps, sets, *rest, **more):
            return project((kept,), steps, sets, *rest, **more)

        slab = jnp.concatenate([mine, others], axis=0)
        z3 = mirrored(slab)
        z1 = neighbours(slab)
        x0 = over_dp(slab, 1)
        y0 = over_dp(slab, 2)
        stacked, facts = stack(doc_blocks, block_mask, plan, own_queries, other_queries)
        slab, x0, y0, other_tokens, stacked, facts = tie(
            slab, x0, y0, other_tokens, stacked, facts
        )
        d0 = over_dp(x0, 2)
        x1 = over_dp(z1, 1)
        y1 = over_dp(z1, 2)
        z2 = neighbours(z3)
        z3, d0 = tie(z3, d0)
        x3 = over_dp(z3, 1)
        y3 = over_dp(z3, 2)
        half = slab.shape[0] // 2

        def diagonal(x, y):
            return over_dp(x[:half], 2), over_dp(y[half:], 1)

        own_sum, kept = multiply((0, 1, 3), [[slab, z1, z3]], last=False, keep=(2, 3))
        d1 = over_dp(y1, 1)
        x2 = over_dp(z2, 1)
        y2 = over_dp(z2, 2)
        own_near = multiply_kept((2,), [[z2]], own_sum)
        own_back = around(own_near, 1)
        own_near, x3, y3 = tie(own_near, x3, y3)
        xy_sum = multiply((0, 1, 3), [[x0, x1, x3], [y0, y1, y3]], last=False)
        xy_sum, x2, y2, x3, y3 = tie(xy_sum, x2, y2, x3, y3)
        d2 = over_dp(x2, 2)
        d3 = diagonal(x3, y3)
        xy_near = multiply_kept((2,), [[x2], [y2]], xy_sum, passed=step_xy, extra=own_back)
        xy_back = around(xy_near, 1)
        d0, d1, xy_near = tie(d0, d1, xy_near)
        d_sum = multiply((0, 1), [[d0, d1]], last=False)
        d_near = multiply_kept((2, 3), [[d2, d3]], d_sum, passed=step_d, extra=xy_back)
        d_back = around(d_near, 1)
        d_far = around(d_back[spare:tall], 1)
    else:
        stacked, facts = stack(doc_blocks, block_mask, plan, own_queries, other_queries)
        even = jnp.where(core == 0, mine, others)
        odd = jnp.where(core == 0, others, mine)
        groups = [list(range(0, size, 2)), list(range(1, size, 2))]
        slab = jnp.concatenate([even, odd], axis=0)
        own_set = lax.all_gather(slab, "ctx", axis=0, axis_index_groups=groups, tiled=True)
        pair_tokens = jnp.where(
            core == 0,
            jnp.concatenate([own_tokens, other_tokens], axis=0),
            jnp.concatenate([other_tokens, own_tokens], axis=0),
        )

        def multiply(sets, passed=(), extra=None):
            parts = [
                jnp.dot(pair_tokens, w, preferred_element_type=jnp.float32).astype(jnp.bfloat16)
                for w in sets
            ]
            parts += [extra[begin:end] for begin, end in passed]
            return jnp.concatenate(parts, axis=0)

        x_set = over_dp(own_set, 1)
        y_set = over_dp(own_set, 2)
        d_set = over_dp(x_set, 2)
        own_near = multiply([own_set])
        own_back = around(own_near, 1)
        xy_near = multiply([x_set, y_set], step_xy, own_back)
        xy_back = around(xy_near, 1)
        d_near = multiply([d_set], step_d, xy_back)
        d_back = around(d_near, 1)
        d_far = around(d_back[spare:tall], 1)

    own_set = (own_near, own_back, xy_back), (0, 0, 2 * tall)
    y_set = (xy_near, xy_back, d_back), (tall, tall, tall + short)
    x_set = (xy_near, xy_back, d_back), (0, 0, tall)
    d_set = (d_near, d_back, d_far), (0, 0, 0)
    near_a = attend_near(0, facts, stacked, own_set, y_set)
    near_b = attend_near(1, facts, stacked, x_set, d_set)
    first = attend_far(0, facts, stacked, near_a, own_set, y_set)
    second = attend_far(1, facts, stacked, near_b, x_set, d_set)
    got_a, got_b = other_core(first[1]), other_core(second[1])
    st_got_a, st_got_b = other_core(first[3]), other_core(second[3])
    vmem = pl.BlockSpec(memory_space=pltpu.VMEM)
    return pl.pallas_call(
        finish_kernel,
        out_shape=(
            jax.ShapeDtypeStruct((1, rows, QH * HD), jnp.bfloat16),
            jax.ShapeDtypeStruct((1, QH, rows), jnp.float32),
        ),
        in_specs=[vmem] * 8,
        out_specs=(vmem, vmem),
        compiler_params=pltpu.CompilerParams(vmem_limit_bytes=VMEM_LIMIT),
    )(first[0], second[0], got_a, got_b, first[2], second[2], st_got_a, st_got_b)


def solution(mesh):
    in_specs = (
        P("dp", "ctx", None),
        P("dp", "ctx", None),
        P("ctx", "dp"),
        P("dp", None),
        P("dp", None, None),
        P("dp", None),
    )
    out_specs = (P("dp", "ctx", None), P("dp", None, "ctx"))
    return jax.shard_map(body, mesh=mesh, in_specs=in_specs, out_specs=out_specs, check_vma=False)
```

```python
import functools
import math

import jax
import jax.numpy as jnp
from jax import lax
from jax.experimental import pallas as pl
from jax.experimental.pallas import tpu as pltpu
from jax.sharding import PartitionSpec as P

HD = 128
QH = 16
KVH = 4
BLK = 128
MAXDOC = 8
GROUP = QH // KVH
LANES = GROUP * BLK
KEPT = (1, 2, 3)
VMEM_LIMIT = 20 * 1024 * 1024
SCALE = 1.0 / math.sqrt(HD)
LOG2E = 1.0 / math.log(2.0)


def over_dp(array, mask):
    return lax.ppermute(array, "dp", [(i, i ^ mask) for i in range(lax.axis_size("dp"))])


def other_core(array):
    return lax.ppermute(array, "ctx", [(i, i ^ 1) for i in range(lax.axis_size("ctx"))])


def around(array, pairs):
    size = lax.axis_size("ctx")
    return lax.ppermute(array, "ctx", [(i, (i + 2 * pairs) % size) for i in range(size)])


def neighbours(array):
    return lax.ppermute(array, "ctx", [(i, i ^ 2) for i in range(lax.axis_size("ctx"))])


def mirrored(array):
    size = lax.axis_size("ctx")
    pairs = [(i, size - 2 - 2 * (i // 2) + i % 2) for i in range(size)]
    return lax.ppermute(array, "ctx", pairs)


def tie(*arrays):
    return lax.optimization_barrier(arrays)


def project_kernel(steps, sets, passed, has_sum, last, keep, depth, *refs):
    refs = list(refs)
    whole = keep is not None
    tokens = [refs.pop(0) for _ in range(2 if whole else 1)]
    weights = []
    for _ in range(len(steps) * sets):
        array = refs.pop(0)
        if array.shape[0] == depth:
            weights.append(((array, 0), (refs.pop(0), 0)))
        else:
            weights.append(((array, 0), (array, depth)))
    kept_ref = refs.pop() if keep else None
    out_ref = refs.pop()
    extras = refs
    device = lax.axis_index("ctx")
    core, pair = device % 2, device // 2
    rows = tokens[0].shape[0] // (1 if whole else 2)

    sources = (pair, pair + 1 - 2 * lax.rem(pair, 2), lax.rem(pair + 2, 4), 3 - pair)

    def group_columns(step, half):
        source = sources[step]
        group = 2 * source + (core + half) % 2
        return pl.ds(pl.multiple_of(group * depth, depth), depth)

    for side in range(2):
        place = core if side == 0 else 1 - core
        here = pl.ds(pl.multiple_of(place * rows, rows), rows)
        if has_sum:
            total = extras[0][here, :]
        else:
            total = jnp.zeros((rows, sets * HD), jnp.float32)
        for position, step in enumerate(steps):
            for half in range(2):
                if whole:
                    piece = tokens[side][:, group_columns(step, half)]
                else:
                    at = (2 * (step - KEPT[0]) + half) * depth
                    piece = tokens[0][side * rows : (side + 1) * rows, at : at + depth]
                parts = [weights[s * len(steps) + position][half] for s in range(sets)]
                weight = jnp.concatenate([array[at : at + depth, :] for array, at in parts], axis=1)
                total += jnp.dot(piece, weight, preferred_element_type=jnp.float32)
        for position, step in enumerate(keep or ()):
            for half in range(2):
                at = (2 * position + half) * depth
                kept_ref[side * rows : (side + 1) * rows, at : at + depth] = tokens[side][
                    :, group_columns(step, half)
                ]
        if not last:
            out_ref[here, :] = total
            continue
        total = total.astype(jnp.bfloat16)
        for s in range(sets):
            at = pl.multiple_of(s * 2 * rows + place * rows, rows)
            out_ref[pl.ds(at, rows), :] = total[:, s * HD : (s + 1) * HD]
    at = sets * 2 * rows
    for begin, end in passed:
        out_ref[at : at + end - begin, :] = extras[-1][begin:end, :]
        at += end - begin


def project(
    tokens, steps, sets, total=None, last=True, passed=(), extra=None, keep=(), cost=1
):
    whole = len(tokens) == 2
    rows = tokens[0].shape[0] * len(tokens)
    weights = []
    for one in sets:
        for w in one:
            weights += w if isinstance(w, tuple) else [w]
    first = sets[0][0]
    depth = first[0].shape[0] if isinstance(first, tuple) else first.shape[0] // 2
    extras = [array for array in (total, extra) if array is not None]
    count = len(sets)
    tall = count * rows + sum(end - begin for begin, end in passed)
    if last:
        out = [jax.ShapeDtypeStruct((tall, HD), jnp.bfloat16)]
    else:
        out = [jax.ShapeDtypeStruct((rows, count * HD), jnp.float32)]
    if keep:
        out.append(jax.ShapeDtypeStruct((rows, len(keep) * 2 * depth), jnp.bfloat16))
    spec = pl.BlockSpec(memory_space=pltpu.VMEM)
    got = pl.pallas_call(
        functools.partial(
            project_kernel,
            steps,
            count,
            passed,
            total is not None,
            last,
            keep if whole else None,
            depth,
        ),
        out_shape=tuple(out),
        in_specs=[spec] * (len(tokens) + len(weights) + len(extras)),
        out_specs=(spec,) * len(out),
        compiler_params=pltpu.CompilerParams(vmem_limit_bytes=VMEM_LIMIT),
        cost_estimate=pl.CostEstimate(
            flops=4 * rows * depth * HD * len(steps) * count * cost,
            bytes_accessed=4 * rows * depth * len(steps) * cost,
            transcendentals=0,
        ),
    )(*tokens, *weights, *extras)
    return got if keep else got[0]


def document_start(docs_ref, block):
    def ends(j, carry):
        end, start = carry
        end = end + docs_ref[0, j]
        return end, jnp.where(end <= block, end, start)

    return lax.fori_loop(0, docs_ref.shape[1], ends, (jnp.int32(0), jnp.int32(0)))[1]


def score_blocks(keys, query, steps, found, causal, table):
    got = lax.dot_general(
        jnp.concatenate([keys(step) for step in steps], axis=0),
        query,
        (((1,), (1,)), ((), ())),
        preferred_element_type=jnp.float32,
    )
    best = None
    for at, step in enumerate(steps):
        part = got[at * BLK : (at + 1) * BLK, :]
        keep = causal if step == 0 and causal is not None else step < found
        part = jnp.where(keep, part, -jnp.inf)
        table[step * BLK : (step + 1) * BLK, :] = part
        best = part if best is None else jnp.maximum(best, part)
    return jnp.max(best, axis=0, keepdims=True)


def weigh_blocks(values, steps, highest, table):
    weights = jnp.exp2(
        (table[steps[0] * BLK : (steps[-1] + 1) * BLK, :] - highest) * (SCALE * LOG2E)
    )
    part = lax.dot_general(
        jnp.concatenate([values(step) for step in steps], axis=0),
        weights.astype(jnp.bfloat16),
        (((0,), (0,)), ((), ())),
        preferred_element_type=jnp.float32,
    )
    return jnp.sum(weights, axis=0, keepdims=True), part


def where_am_i(second):
    device = lax.axis_index("ctx")
    slice_of = lax.axis_index("dp")
    core, pair = device % 2, device // 2
    column, kind = slice_of % 2, slice_of // 2
    return core, pair, kind, 2 * ((column + second) % 2) + core


def stack_kernel(docs_ref, mask_ref, plan_ref, q_own_ref, q_other_ref, out_ref, facts):
    core, pair, _, _ = where_am_i(0)
    blocks = q_own_ref.shape[0] // BLK
    for side in range(2):
        for place in range(blocks):
            item = side * blocks + place
            index = (core if side == 0 else 1 - core) * blocks + place
            block = 2 * blocks * pair + index
            start = document_start(docs_ref, block)
            for back in range(1, MAXDOC):
                admitted = jnp.logical_and(
                    block - back >= start, mask_ref[0, block, back - 1] == 1
                )
                facts[item, back] = admitted.astype(jnp.int32)
            facts[item, 0] = index
            facts[item, MAXDOC] = plan_ref[0, block] - 2 * blocks * pair
    for second in range(2):
        head = where_am_i(second)[3]
        columns = pl.ds(pl.multiple_of(head * LANES, LANES), LANES)
        for side, q_ref in enumerate((q_own_ref, q_other_ref)):
            for place in range(blocks):
                query = q_ref[place * BLK : (place + 1) * BLK, columns]
                for g in range(GROUP):
                    out_ref[second, side * blocks + place, g * BLK : (g + 1) * BLK, :] = query[
                        :, g * HD : (g + 1) * HD
                    ]


def stack(docs, mask, plan, q_own, q_other):
    vmem = pl.BlockSpec(memory_space=pltpu.VMEM)
    smem = pl.BlockSpec(memory_space=pltpu.SMEM)
    items = 2 * q_own.shape[0] // BLK
    return pl.pallas_call(
        stack_kernel,
        out_shape=(
            jax.ShapeDtypeStruct((2, items, LANES, HD), jnp.bfloat16),
            jax.ShapeDtypeStruct((items, MAXDOC + 1), jnp.int32),
        ),
        in_specs=[smem] * 3 + [vmem] * 2,
        out_specs=(vmem, smem),
        compiler_params=pltpu.CompilerParams(vmem_limit_bytes=VMEM_LIMIT),
        cost_estimate=pl.CostEstimate(
            flops=0, bytes_accessed=4 * items * LANES * HD, transcendentals=0
        ),
    )(docs, mask, plan, q_own, q_other)


def near_kernel(
    second,
    starts,
    facts,
    queries_ref,
    near_a,
    near_b,
    back_a,
    back_b,
    summed,
    stat,
    kv,
    table,
    places,
):
    kind = where_am_i(second)[2]
    pair_blocks = queries_ref.shape[1]
    tall = pair_blocks * BLK
    for which, near, back, at in (
        (kind, near_a, back_a, starts[0]),
        (1 - kind, near_b, back_b, starts[1]),
    ):
        kv[which, :tall, :] = back[at[1] : at[1] + tall, :]
        kv[which, tall:, :] = near[at[0] : at[0] + tall, :]
    causal = lax.broadcasted_iota(jnp.int32, (BLK, BLK), 0) <= lax.broadcasted_iota(
        jnp.int32, (BLK, BLK), 1
    )
    causal = jnp.tile(causal, (1, GROUP))

    for item in range(pair_blocks):
        index = facts[item, 0]
        for step in range(MAXDOC + 1):
            places[step] = tall + index * BLK
        found = jnp.int32(1)
        for back in range(1, MAXDOC):
            places[found] = tall + (index - back) * BLK
            found += jnp.where(back <= index + pair_blocks, facts[item, back], 0)
        places[found] = tall + index * BLK
        rows = queries_ref[second, item]

        def fetch(which, step):
            return kv[which, pl.ds(pl.multiple_of(places[step], BLK), BLK), :]

        keys = functools.partial(fetch, 0)
        values = functools.partial(fetch, 1)
        half = MAXDOC // 2
        low, high = range(half), range(half, MAXDOC)
        stat[item, 0:1, :] = score_blocks(keys, rows, low, found, causal, table)

        few = jnp.logical_and(found > half, found <= half + 2)
        many = found > half + 2

        def score_rest(steps):
            stat[item, 0:1, :] = jnp.maximum(
                stat[item, 0:1, :], score_blocks(keys, rows, steps, found, None, table)
            )

        def weigh_rest(steps):
            more, part = weigh_blocks(values, steps, stat[item, 0:1, :], table)
            stat[item, 1:2, :] += more
            summed[item] += part

        pl.when(few)(functools.partial(score_rest, high[:2]))
        pl.when(many)(functools.partial(score_rest, high))
        stat[item, 1:2, :], summed[item] = weigh_blocks(values, low, stat[item, 0:1, :], table)

        pl.when(few)(functools.partial(weigh_rest, high[:2]))
        pl.when(many)(functools.partial(weigh_rest, high))


def far_kernel(
    second,
    starts,
    facts,
    summed_ref,
    stat_ref,
    queries_ref,
    far_a,
    far_b,
    *refs,
):
    before_own, before_other = refs[:2] if second else (None, None)
    (
        out_own,
        out_other,
        stats_own,
        stats_other,
        kv,
        table,
        top,
        total,
        summed,
        places,
    ) = refs[2 * second :]
    core, _, kind, _ = where_am_i(second)
    if second:
        dev = before_own.shape[0]
        stats_own[dev:, :, :] = before_own[...]
        stats_other[dev:, :, :] = before_other[...]
    pair_blocks = queries_ref.shape[1]
    dev_blocks = pair_blocks // 2
    far_blocks = (MAXDOC - 1) % pair_blocks
    short = far_blocks * BLK
    for which, far, at in ((kind, far_a, starts[0]), (1 - kind, far_b, starts[1])):
        kv[which, :, :] = far[at[2] : at[2] + short, :]

    for item in range(pair_blocks):
        side, place = divmod(item, dev_blocks)
        out_ref = (out_own, out_other)[side]
        rows = slice(place * BLK, (place + 1) * BLK)
        index = facts[item, 0]
        for step in range(far_blocks + 1):
            places[step] = 0
        found = jnp.int32(0)
        for back in range(MAXDOC - far_blocks, MAXDOC):
            places[found] = (far_blocks + pair_blocks + index - back) * BLK
            found += jnp.where(back > index + pair_blocks, facts[item, back], 0)
        places[found] = 0
        top[...] = stat_ref[item, 0:1, :]
        total[...] = stat_ref[item, 1:2, :]
        summed[...] = summed_ref[item]

        @pl.when(found > 0)
        def _():
            query = queries_ref[second, item]

            def fetch(which, step):
                return kv[which, pl.ds(pl.multiple_of(places[step], BLK), BLK), :]

            steps = range(far_blocks)
            before = top[...]
            highest = jnp.maximum(
                before,
                score_blocks(functools.partial(fetch, 0), query, steps, found, None, table),
            )
            more, part = weigh_blocks(functools.partial(fetch, 1), steps, highest, table)
            shrink = jnp.exp2((before - highest) * (SCALE * LOG2E))
            top[...] = highest
            total[...] = total[...] * shrink + more
            summed[...] = summed[...] * shrink + part

        result = summed[...] / total[...]
        for g in range(GROUP):
            out_ref[rows, g * HD : (g + 1) * HD] = (
                result[:, g * BLK : (g + 1) * BLK].T.astype(jnp.bfloat16)
            )
        lse = top[...] * SCALE + jnp.log(total[...])
        slot = facts[item, MAXDOC]
        keep_here = slot // dev_blocks == core
        slot_at = slot % dev_blocks

        @pl.when(keep_here)
        def _():
            for g in range(GROUP):
                stats_own[slot_at, g : g + 1, :] = lse[:, g * BLK : (g + 1) * BLK]

        @pl.when(jnp.logical_not(keep_here))
        def _():
            for g in range(GROUP):
                stats_other[slot_at, g : g + 1, :] = lse[:, g * BLK : (g + 1) * BLK]


def attend_near(second, facts, queries, first_set, second_set):
    vmem = pl.BlockSpec(memory_space=pltpu.VMEM)
    smem = pl.BlockSpec(memory_space=pltpu.SMEM)
    items = queries.shape[1]
    (near_a, back_a, _), start_a = first_set
    (near_b, back_b, _), start_b = second_set
    return pl.pallas_call(
        functools.partial(near_kernel, second, (start_a, start_b)),
        out_shape=(
            jax.ShapeDtypeStruct((items, HD, LANES), jnp.float32),
            jax.ShapeDtypeStruct((items, 8, LANES), jnp.float32),
        ),
        in_specs=[smem] + [vmem] * 5,
        out_specs=(vmem,) * 2,
        scratch_shapes=[
            pltpu.VMEM((2, 2 * items * BLK, HD), jnp.bfloat16),
            pltpu.VMEM((MAXDOC * BLK, LANES), jnp.float32),
            pltpu.SMEM((MAXDOC + 1,), jnp.int32),
        ],
        compiler_params=pltpu.CompilerParams(vmem_limit_bytes=VMEM_LIMIT),
        cost_estimate=pl.CostEstimate(
            flops=items * MAXDOC * BLK * LANES * HD * 4,
            bytes_accessed=4 * items * BLK * QH * HD,
            transcendentals=items * MAXDOC * BLK * LANES,
        ),
    )(facts, queries, near_a, near_b, back_a, back_b)


def attend_far(second, facts, queries, carried, first_set, second_set, before=()):
    vmem = pl.BlockSpec(memory_space=pltpu.VMEM)
    smem = pl.BlockSpec(memory_space=pltpu.SMEM)
    items = queries.shape[1]
    dev_blocks = items // 2
    rows = dev_blocks * BLK
    far_blocks = (MAXDOC - 1) % items
    (_, _, far_a), start_a = first_set
    (_, _, far_b), start_b = second_set
    out = jax.ShapeDtypeStruct((rows, LANES), jnp.bfloat16)
    stats = jax.ShapeDtypeStruct(((1 + second) * dev_blocks, GROUP, BLK), jnp.float32)
    return pl.pallas_call(
        functools.partial(far_kernel, second, (start_a, start_b)),
        out_shape=(out, out, stats, stats),
        in_specs=[smem] + [vmem] * (5 + len(before)),
        out_specs=(vmem,) * 4,
        scratch_shapes=[
            pltpu.VMEM((2, far_blocks * BLK, HD), jnp.bfloat16),
            pltpu.VMEM((far_blocks * BLK, LANES), jnp.float32),
            pltpu.VMEM((1, LANES), jnp.float32),
            pltpu.VMEM((1, LANES), jnp.float32),
            pltpu.VMEM((HD, LANES), jnp.float32),
            pltpu.SMEM((far_blocks + 1,), jnp.int32),
        ],
        compiler_params=pltpu.CompilerParams(vmem_limit_bytes=VMEM_LIMIT),
        cost_estimate=pl.CostEstimate(
            flops=items * far_blocks * BLK * LANES * HD * 4,
            bytes_accessed=8 * rows * LANES,
            transcendentals=items * far_blocks * BLK * LANES,
        ),
    )(facts, *carried, queries, far_a, far_b, *before)


def finish_kernel(own_a, own_b, got_a, got_b, st_own, st_got, out_ref, stats_ref):
    core = lax.axis_index("ctx") % 2
    column = lax.axis_index("dp") % 2
    pieces = (
        (own_a, column, core),
        (own_b, 1 - column, core),
        (got_a, column, 1 - core),
        (got_b, 1 - column, 1 - core),
    )
    for piece, head_pair, side in pieces:
        head = 2 * head_pair + side
        out_ref[0, :, pl.ds(pl.multiple_of(head * LANES, LANES), LANES)] = piece[...]
    for head in range(KVH):
        is_a = head // 2 == column
        is_own = head % 2 == core
        both = jnp.where(is_own, st_own[...], st_got[...])
        lse = jnp.where(is_a, both[both.shape[0] // 2 :], both[: both.shape[0] // 2])
        for place in range(lse.shape[0]):
            stats_ref[0, head * GROUP : (head + 1) * GROUP, place * BLK : (place + 1) * BLK] = lse[place]


def body(tokens, queries, kv_weight, doc_blocks, block_mask, plan):
    size = lax.axis_size("ctx")
    device = lax.axis_index("ctx")
    core = device % 2
    slots = size // 2
    own_tokens, own_queries = tokens[0], queries[0]
    rows = own_tokens.shape[0]
    other_weight = other_core(kv_weight)
    other_weight, own_tokens, own_queries = tie(other_weight, own_tokens, own_queries)
    other_queries = other_core(own_queries)

    def my_half(array):
        return lax.dynamic_slice_in_dim(array, core * HD, HD, 1)

    other_tokens = other_core(own_tokens)
    mine = my_half(kv_weight)
    others = my_half(other_weight)
    tall = 2 * rows
    spare = tall - (MAXDOC - 1) % (tall // BLK) * BLK
    short = tall - spare
    step_xy = ((spare, tall),)
    if slots == 4:

        def multiply(steps, sets, *rest, **more):
            return project((own_tokens, other_tokens), steps, sets, *rest, **more)

        def multiply_kept(steps, sets, *rest, **more):
            return project((kept,), steps, sets, *rest, **more)

        slab = jnp.concatenate([mine, others], axis=0)
        z3 = mirrored(slab)
        z1 = neighbours(slab)
        x0 = over_dp(slab, 1)
        y0 = over_dp(slab, 2)
        stacked, facts = stack(doc_blocks, block_mask, plan, own_queries, other_queries)
        slab, x0, y0, other_tokens, stacked, facts = tie(
            slab, x0, y0, other_tokens, stacked, facts
        )
        d0 = over_dp(x0, 2)
        x1 = over_dp(z1, 1)
        y1 = over_dp(z1, 2)
        z2 = neighbours(z3)
        z3, d0 = tie(z3, d0)
        x3 = over_dp(z3, 1)
        y3 = over_dp(z3, 2)
        half = slab.shape[0] // 2

        def diagonal(x, y):
            return over_dp(x[:half], 2), over_dp(y[half:], 1)

        own_sum, kept = multiply((0, 1, 3), [[slab, z1, z3]], last=False, keep=KEPT)
        d1 = over_dp(y1, 1)
        x2 = over_dp(z2, 1)
        y2 = over_dp(z2, 2)
        own_near = multiply_kept((2,), [[z2]], own_sum)
        own_back = around(own_near, 1)
        own_near, x3, y3 = tie(own_near, x3, y3)
        xy_sum = multiply((0, 1, 3), [[x0, x1, x3], [y0, y1, y3]], last=False)
        xy_sum, x2, y2, x3, y3 = tie(xy_sum, x2, y2, x3, y3)
        d2 = over_dp(x2, 2)
        d3 = diagonal(x3, y3)
        xy_near = multiply_kept(
            (2,), [[x2], [y2]], xy_sum, passed=step_xy, extra=own_back, cost=0
        )
        xy_back = around(xy_near, 1)
        d_sum = multiply((0,), [[d0]], last=False, cost=0)
        xy_far = around(xy_back[spare : 2 * tall], 1)
        d_near = multiply_kept((1, 2, 3), [[d1, d2, d3]], d_sum)
        d_back = around(d_near, 1)
        d_far = around(d_back[spare:], 1)
    else:
        stacked, facts = stack(doc_blocks, block_mask, plan, own_queries, other_queries)
        even = jnp.where(core == 0, mine, others)
        odd = jnp.where(core == 0, others, mine)
        groups = [list(range(0, size, 2)), list(range(1, size, 2))]
        slab = jnp.concatenate([even, odd], axis=0)
        own_set = lax.all_gather(slab, "ctx", axis=0, axis_index_groups=groups, tiled=True)
        pair_tokens = jnp.where(
            core == 0,
            jnp.concatenate([own_tokens, other_tokens], axis=0),
            jnp.concatenate([other_tokens, own_tokens], axis=0),
        )

        def multiply(sets, passed=(), extra=None):
            parts = [
                jnp.dot(pair_tokens, w, preferred_element_type=jnp.float32).astype(jnp.bfloat16)
                for w in sets
            ]
            parts += [extra[begin:end] for begin, end in passed]
            return jnp.concatenate(parts, axis=0)

        x_set = over_dp(own_set, 1)
        y_set = over_dp(own_set, 2)
        d_set = over_dp(x_set, 2)
        own_near = multiply([own_set])
        own_back = around(own_near, 1)
        xy_near = multiply([x_set, y_set], step_xy, own_back)
        xy_back = around(xy_near, 1)
        d_near = multiply([d_set])
        xy_far = around(xy_back[spare : 2 * tall], 1)
        d_back = around(d_near, 1)
        d_far = around(d_back[spare:], 1)

    own_set = (own_near, own_back, xy_back), (0, 0, 2 * tall)
    y_set = (xy_near, xy_back, xy_far), (tall, tall, tall)
    x_set = (xy_near, xy_back, xy_far), (0, 0, 0)
    d_set = (d_near, d_back, d_far), (0, 0, 0)
    near_a = attend_near(0, facts, stacked, own_set, y_set)
    near_b = attend_near(1, facts, stacked, x_set, d_set)
    first = attend_far(0, facts, stacked, near_a, own_set, y_set)
    second = attend_far(1, facts, stacked, near_b, x_set, d_set, first[2:])
    got_a, got_b = other_core(first[1]), other_core(second[1])
    st_got = other_core(second[3])
    vmem = pl.BlockSpec(memory_space=pltpu.VMEM)
    return pl.pallas_call(
        finish_kernel,
        out_shape=(
            jax.ShapeDtypeStruct((1, rows, QH * HD), jnp.bfloat16),
            jax.ShapeDtypeStruct((1, QH, rows), jnp.float32),
        ),
        in_specs=[vmem] * 6,
        out_specs=(vmem, vmem),
        compiler_params=pltpu.CompilerParams(vmem_limit_bytes=VMEM_LIMIT),
    )(first[0], second[0], got_a, got_b, second[2], st_got)


def solution(mesh):
    in_specs = (
        P("dp", "ctx", None),
        P("dp", "ctx", None),
        P("ctx", "dp"),
        P("dp", None),
        P("dp", None, None),
        P("dp", None),
    )
    out_specs = (P("dp", "ctx", None), P("dp", None, "ctx"))
    return jax.shard_map(body, mesh=mesh, in_specs=in_specs, out_specs=out_specs, check_vma=False)
```

```python
import functools
import math

import jax
import jax.numpy as jnp
from jax import lax
from jax.experimental import pallas as pl
from jax.experimental.pallas import tpu as pltpu
from jax.sharding import PartitionSpec as P

HD = 128
QH = 16
KVH = 4
BLK = 128
MAXDOC = 8
GROUP = QH // KVH
LANES = GROUP * BLK
KEPT = (1, 2, 3)
VMEM_LIMIT = 20 * 1024 * 1024
SCALE = 1.0 / math.sqrt(HD)
LOG2E = 1.0 / math.log(2.0)


def over_dp(array, mask):
    return lax.ppermute(array, "dp", [(i, i ^ mask) for i in range(lax.axis_size("dp"))])


def other_core(array):
    return lax.ppermute(array, "ctx", [(i, i ^ 1) for i in range(lax.axis_size("ctx"))])


def around(array, pairs):
    size = lax.axis_size("ctx")
    return lax.ppermute(array, "ctx", [(i, (i + 2 * pairs) % size) for i in range(size)])


def neighbours(array):
    return lax.ppermute(array, "ctx", [(i, i ^ 2) for i in range(lax.axis_size("ctx"))])


def mirrored(array):
    size = lax.axis_size("ctx")
    pairs = [(i, size - 2 - 2 * (i // 2) + i % 2) for i in range(size)]
    return lax.ppermute(array, "ctx", pairs)


def tie(*arrays):
    return lax.optimization_barrier(arrays)


def project_kernel(steps, sets, passed, has_sum, last, keep, depth, *refs):
    refs = list(refs)
    whole = keep is not None
    tokens = [refs.pop(0) for _ in range(2 if whole else 1)]
    weights = []
    for _ in range(len(steps) * sets):
        array = refs.pop(0)
        if array.shape[0] == depth:
            weights.append(((array, 0), (refs.pop(0), 0)))
        else:
            weights.append(((array, 0), (array, depth)))
    kept_ref = refs.pop() if keep else None
    out_ref = refs.pop()
    extras = refs
    device = lax.axis_index("ctx")
    core, pair = device % 2, device // 2
    rows = tokens[0].shape[0] // (1 if whole else 2)

    sources = (pair, pair + 1 - 2 * lax.rem(pair, 2), lax.rem(pair + 2, 4), 3 - pair)

    def group_columns(step, half):
        source = sources[step]
        group = 2 * source + (core + half) % 2
        return pl.ds(pl.multiple_of(group * depth, depth), depth)

    for side in range(2):
        place = core if side == 0 else 1 - core
        here = pl.ds(pl.multiple_of(place * rows, rows), rows)
        if has_sum:
            total = extras[0][here, :]
        else:
            total = jnp.zeros((rows, sets * HD), jnp.float32)
        for position, step in enumerate(steps):
            for half in range(2):
                if whole:
                    piece = tokens[side][:, group_columns(step, half)]
                else:
                    at = (2 * (step - KEPT[0]) + half) * depth
                    piece = tokens[0][side * rows : (side + 1) * rows, at : at + depth]
                parts = [weights[s * len(steps) + position][half] for s in range(sets)]
                weight = jnp.concatenate([array[at : at + depth, :] for array, at in parts], axis=1)
                total += jnp.dot(piece, weight, preferred_element_type=jnp.float32)
        for position, step in enumerate(keep or ()):
            for half in range(2):
                at = (2 * position + half) * depth
                kept_ref[side * rows : (side + 1) * rows, at : at + depth] = tokens[side][
                    :, group_columns(step, half)
                ]
        if not last:
            out_ref[here, :] = total
            continue
        total = total.astype(jnp.bfloat16)
        for s in range(sets):
            at = pl.multiple_of(s * 2 * rows + place * rows, rows)
            out_ref[pl.ds(at, rows), :] = total[:, s * HD : (s + 1) * HD]
    at = sets * 2 * rows
    for begin, end in passed:
        out_ref[at : at + end - begin, :] = extras[-1][begin:end, :]
        at += end - begin


def project(
    tokens, steps, sets, total=None, last=True, passed=(), extra=None, keep=(), cost=1
):
    whole = len(tokens) == 2
    rows = tokens[0].shape[0] * len(tokens)
    weights = []
    for one in sets:
        for w in one:
            weights += w if isinstance(w, tuple) else [w]
    first = sets[0][0]
    depth = first[0].shape[0] if isinstance(first, tuple) else first.shape[0] // 2
    extras = [array for array in (total, extra) if array is not None]
    count = len(sets)
    tall = count * rows + sum(end - begin for begin, end in passed)
    if last:
        out = [jax.ShapeDtypeStruct((tall, HD), jnp.bfloat16)]
    else:
        out = [jax.ShapeDtypeStruct((rows, count * HD), jnp.float32)]
    if keep:
        out.append(jax.ShapeDtypeStruct((rows, len(keep) * 2 * depth), jnp.bfloat16))
    spec = pl.BlockSpec(memory_space=pltpu.VMEM)
    got = pl.pallas_call(
        functools.partial(
            project_kernel,
            steps,
            count,
            passed,
            total is not None,
            last,
            keep if whole else None,
            depth,
        ),
        out_shape=tuple(out),
        in_specs=[spec] * (len(tokens) + len(weights) + len(extras)),
        out_specs=(spec,) * len(out),
        compiler_params=pltpu.CompilerParams(vmem_limit_bytes=VMEM_LIMIT),
        cost_estimate=pl.CostEstimate(
            flops=4 * rows * depth * HD * len(steps) * count * cost,
            bytes_accessed=4 * rows * depth * len(steps) * cost,
            transcendentals=0,
        ),
    )(*tokens, *weights, *extras)
    return got if keep else got[0]


def document_start(docs_ref, block):
    def ends(j, carry):
        end, start = carry
        end = end + docs_ref[0, j]
        return end, jnp.where(end <= block, end, start)

    return lax.fori_loop(0, docs_ref.shape[1], ends, (jnp.int32(0), jnp.int32(0)))[1]


def score_blocks(keys, query, steps, found, causal, table):
    got = lax.dot_general(
        jnp.concatenate([keys(step) for step in steps], axis=0),
        query,
        (((1,), (1,)), ((), ())),
        preferred_element_type=jnp.float32,
    )
    best = None
    for at, step in enumerate(steps):
        part = got[at * BLK : (at + 1) * BLK, :]
        keep = causal if step == 0 and causal is not None else step < found
        part = jnp.where(keep, part, -jnp.inf)
        table[step * BLK : (step + 1) * BLK, :] = part
        best = part if best is None else jnp.maximum(best, part)
    return jnp.max(best, axis=0, keepdims=True)


def weigh_blocks(values, steps, highest, table):
    weights = jnp.exp2(
        (table[steps[0] * BLK : (steps[-1] + 1) * BLK, :] - highest) * (SCALE * LOG2E)
    )
    part = lax.dot_general(
        jnp.concatenate([values(step) for step in steps], axis=0),
        weights.astype(jnp.bfloat16),
        (((0,), (0,)), ((), ())),
        preferred_element_type=jnp.float32,
    )
    return jnp.sum(weights, axis=0, keepdims=True), part


def where_am_i(second):
    device = lax.axis_index("ctx")
    slice_of = lax.axis_index("dp")
    core, pair = device % 2, device // 2
    column, kind = slice_of % 2, slice_of // 2
    return core, pair, kind, 2 * ((column + second) % 2) + core


def stack_kernel(docs_ref, mask_ref, plan_ref, q_own_ref, q_other_ref, out_ref, facts):
    core, pair, _, _ = where_am_i(0)
    blocks = q_own_ref.shape[0] // BLK
    for side in range(2):
        for place in range(blocks):
            item = side * blocks + place
            index = (core if side == 0 else 1 - core) * blocks + place
            block = 2 * blocks * pair + index
            start = document_start(docs_ref, block)
            for back in range(1, MAXDOC):
                admitted = jnp.logical_and(
                    block - back >= start, mask_ref[0, block, back - 1] == 1
                )
                facts[item, back] = admitted.astype(jnp.int32)
            facts[item, 0] = index
            facts[item, MAXDOC] = plan_ref[0, block] - 2 * blocks * pair
    for second in range(2):
        head = where_am_i(second)[3]
        columns = pl.ds(pl.multiple_of(head * LANES, LANES), LANES)
        for side, q_ref in enumerate((q_own_ref, q_other_ref)):
            for place in range(blocks):
                query = q_ref[place * BLK : (place + 1) * BLK, columns]
                for g in range(GROUP):
                    out_ref[second, side * blocks + place, g * BLK : (g + 1) * BLK, :] = query[
                        :, g * HD : (g + 1) * HD
                    ]


def stack(docs, mask, plan, q_own, q_other):
    vmem = pl.BlockSpec(memory_space=pltpu.VMEM)
    smem = pl.BlockSpec(memory_space=pltpu.SMEM)
    items = 2 * q_own.shape[0] // BLK
    return pl.pallas_call(
        stack_kernel,
        out_shape=(
            jax.ShapeDtypeStruct((2, items, LANES, HD), jnp.bfloat16),
            jax.ShapeDtypeStruct((items, MAXDOC + 1), jnp.int32),
        ),
        in_specs=[smem] * 3 + [vmem] * 2,
        out_specs=(vmem, smem),
        compiler_params=pltpu.CompilerParams(vmem_limit_bytes=VMEM_LIMIT),
        cost_estimate=pl.CostEstimate(
            flops=0, bytes_accessed=4 * items * LANES * HD, transcendentals=0
        ),
    )(docs, mask, plan, q_own, q_other)


def near_kernel(
    second,
    starts,
    facts,
    queries_ref,
    near_a,
    near_b,
    back_a,
    back_b,
    summed,
    stat,
    kv,
    table,
    places,
):
    kind = where_am_i(second)[2]
    pair_blocks = queries_ref.shape[1]
    tall = pair_blocks * BLK
    for which, near, back, at in (
        (kind, near_a, back_a, starts[0]),
        (1 - kind, near_b, back_b, starts[1]),
    ):
        kv[which, :tall, :] = back[at[1] : at[1] + tall, :]
        kv[which, tall:, :] = near[at[0] : at[0] + tall, :]
    causal = lax.broadcasted_iota(jnp.int32, (BLK, BLK), 0) <= lax.broadcasted_iota(
        jnp.int32, (BLK, BLK), 1
    )
    causal = jnp.tile(causal, (1, GROUP))

    for item in range(pair_blocks):
        index = facts[item, 0]
        for step in range(MAXDOC + 1):
            places[step] = tall + index * BLK
        found = jnp.int32(1)
        for back in range(1, MAXDOC):
            places[found] = tall + (index - back) * BLK
            found += jnp.where(back <= index + pair_blocks, facts[item, back], 0)
        places[found] = tall + index * BLK
        rows = queries_ref[second, item]

        def fetch(which, step):
            return kv[which, pl.ds(pl.multiple_of(places[step], BLK), BLK), :]

        keys = functools.partial(fetch, 0)
        values = functools.partial(fetch, 1)
        half = MAXDOC // 2
        low, high = range(half), range(half, MAXDOC)
        stat[item, 0:1, :] = score_blocks(keys, rows, low, found, causal, table)

        def score_rest(steps):
            stat[item, 0:1, :] = jnp.maximum(
                stat[item, 0:1, :], score_blocks(keys, rows, steps, found, None, table)
            )

        def weigh_rest(steps):
            more, part = weigh_blocks(values, steps, stat[item, 0:1, :], table)
            stat[item, 1:2, :] += more
            summed[item] += part

        for more_blocks in range(1, MAXDOC - half + 1):
            pl.when(found == half + more_blocks)(
                functools.partial(score_rest, high[:more_blocks])
            )
        stat[item, 1:2, :], summed[item] = weigh_blocks(values, low, stat[item, 0:1, :], table)

        for more_blocks in range(1, MAXDOC - half + 1):
            pl.when(found == half + more_blocks)(
                functools.partial(weigh_rest, high[:more_blocks])
            )


def far_kernel(
    second,
    starts,
    facts,
    summed_ref,
    stat_ref,
    queries_ref,
    far_a,
    far_b,
    *refs,
):
    before_own, before_other = refs[:2] if second else (None, None)
    (
        out_own,
        out_other,
        stats_own,
        stats_other,
        kv,
        table,
        top,
        total,
        summed,
        places,
    ) = refs[2 * second :]
    core, _, kind, _ = where_am_i(second)
    if second:
        dev = before_own.shape[0]
        stats_own[dev:, :, :] = before_own[...]
        stats_other[dev:, :, :] = before_other[...]
    pair_blocks = queries_ref.shape[1]
    dev_blocks = pair_blocks // 2
    far_blocks = (MAXDOC - 1) % pair_blocks
    short = far_blocks * BLK
    for which, far, at in ((kind, far_a, starts[0]), (1 - kind, far_b, starts[1])):
        kv[which, :, :] = far[at[2] : at[2] + short, :]

    for item in range(pair_blocks):
        side, place = divmod(item, dev_blocks)
        out_ref = (out_own, out_other)[side]
        rows = slice(place * BLK, (place + 1) * BLK)
        index = facts[item, 0]
        for step in range(far_blocks + 1):
            places[step] = 0
        found = jnp.int32(0)
        for back in range(MAXDOC - far_blocks, MAXDOC):
            places[found] = (far_blocks + pair_blocks + index - back) * BLK
            found += jnp.where(back > index + pair_blocks, facts[item, back], 0)
        places[found] = 0
        top[...] = stat_ref[item, 0:1, :]
        total[...] = stat_ref[item, 1:2, :]
        summed[...] = summed_ref[item]

        @pl.when(found > 0)
        def _():
            query = queries_ref[second, item]

            def fetch(which, step):
                return kv[which, pl.ds(pl.multiple_of(places[step], BLK), BLK), :]

            steps = range(far_blocks)
            before = top[...]
            highest = jnp.maximum(
                before,
                score_blocks(functools.partial(fetch, 0), query, steps, found, None, table),
            )
            more, part = weigh_blocks(functools.partial(fetch, 1), steps, highest, table)
            shrink = jnp.exp2((before - highest) * (SCALE * LOG2E))
            top[...] = highest
            total[...] = total[...] * shrink + more
            summed[...] = summed[...] * shrink + part

        result = summed[...] / total[...]
        for g in range(GROUP):
            out_ref[rows, g * HD : (g + 1) * HD] = (
                result[:, g * BLK : (g + 1) * BLK].T.astype(jnp.bfloat16)
            )
        lse = top[...] * SCALE + jnp.log(total[...])
        slot = facts[item, MAXDOC]
        keep_here = slot // dev_blocks == core
        slot_at = slot % dev_blocks

        @pl.when(keep_here)
        def _():
            for g in range(GROUP):
                stats_own[slot_at, g : g + 1, :] = lse[:, g * BLK : (g + 1) * BLK]

        @pl.when(jnp.logical_not(keep_here))
        def _():
            for g in range(GROUP):
                stats_other[slot_at, g : g + 1, :] = lse[:, g * BLK : (g + 1) * BLK]


def attend_near(second, facts, queries, first_set, second_set):
    vmem = pl.BlockSpec(memory_space=pltpu.VMEM)
    smem = pl.BlockSpec(memory_space=pltpu.SMEM)
    items = queries.shape[1]
    (near_a, back_a, _), start_a = first_set
    (near_b, back_b, _), start_b = second_set
    return pl.pallas_call(
        functools.partial(near_kernel, second, (start_a, start_b)),
        out_shape=(
            jax.ShapeDtypeStruct((items, HD, LANES), jnp.float32),
            jax.ShapeDtypeStruct((items, 8, LANES), jnp.float32),
        ),
        in_specs=[smem] + [vmem] * 5,
        out_specs=(vmem,) * 2,
        scratch_shapes=[
            pltpu.VMEM((2, 2 * items * BLK, HD), jnp.bfloat16),
            pltpu.VMEM((MAXDOC * BLK, LANES), jnp.float32),
            pltpu.SMEM((MAXDOC + 1,), jnp.int32),
        ],
        compiler_params=pltpu.CompilerParams(vmem_limit_bytes=VMEM_LIMIT),
        cost_estimate=pl.CostEstimate(
            flops=items * MAXDOC * BLK * LANES * HD * 4,
            bytes_accessed=4 * items * BLK * QH * HD,
            transcendentals=items * MAXDOC * BLK * LANES,
        ),
    )(facts, queries, near_a, near_b, back_a, back_b)


def attend_far(second, facts, queries, carried, first_set, second_set, before=()):
    vmem = pl.BlockSpec(memory_space=pltpu.VMEM)
    smem = pl.BlockSpec(memory_space=pltpu.SMEM)
    items = queries.shape[1]
    dev_blocks = items // 2
    rows = dev_blocks * BLK
    far_blocks = (MAXDOC - 1) % items
    (_, _, far_a), start_a = first_set
    (_, _, far_b), start_b = second_set
    out = jax.ShapeDtypeStruct((rows, LANES), jnp.bfloat16)
    stats = jax.ShapeDtypeStruct(((1 + second) * dev_blocks, GROUP, BLK), jnp.float32)
    return pl.pallas_call(
        functools.partial(far_kernel, second, (start_a, start_b)),
        out_shape=(out, out, stats, stats),
        in_specs=[smem] + [vmem] * (5 + len(before)),
        out_specs=(vmem,) * 4,
        scratch_shapes=[
            pltpu.VMEM((2, far_blocks * BLK, HD), jnp.bfloat16),
            pltpu.VMEM((far_blocks * BLK, LANES), jnp.float32),
            pltpu.VMEM((1, LANES), jnp.float32),
            pltpu.VMEM((1, LANES), jnp.float32),
            pltpu.VMEM((HD, LANES), jnp.float32),
            pltpu.SMEM((far_blocks + 1,), jnp.int32),
        ],
        compiler_params=pltpu.CompilerParams(vmem_limit_bytes=VMEM_LIMIT),
        cost_estimate=pl.CostEstimate(
            flops=items * far_blocks * BLK * LANES * HD * 4,
            bytes_accessed=8 * rows * LANES,
            transcendentals=items * far_blocks * BLK * LANES,
        ),
    )(facts, *carried, queries, far_a, far_b, *before)


def finish_kernel(own_a, own_b, got_a, got_b, st_own, st_got, out_ref, stats_ref):
    core = lax.axis_index("ctx") % 2
    column = lax.axis_index("dp") % 2
    pieces = (
        (own_a, column, core),
        (own_b, 1 - column, core),
        (got_a, column, 1 - core),
        (got_b, 1 - column, 1 - core),
    )
    for piece, head_pair, side in pieces:
        head = 2 * head_pair + side
        out_ref[0, :, pl.ds(pl.multiple_of(head * LANES, LANES), LANES)] = piece[...]
    for head in range(KVH):
        is_a = head // 2 == column
        is_own = head % 2 == core
        both = jnp.where(is_own, st_own[...], st_got[...])
        lse = jnp.where(is_a, both[both.shape[0] // 2 :], both[: both.shape[0] // 2])
        for place in range(lse.shape[0]):
            stats_ref[0, head * GROUP : (head + 1) * GROUP, place * BLK : (place + 1) * BLK] = lse[place]


def body(tokens, queries, kv_weight, doc_blocks, block_mask, plan):
    size = lax.axis_size("ctx")
    device = lax.axis_index("ctx")
    core = device % 2
    slots = size // 2
    own_tokens, own_queries = tokens[0], queries[0]
    rows = own_tokens.shape[0]
    other_weight = other_core(kv_weight)
    other_weight, own_tokens, own_queries = tie(other_weight, own_tokens, own_queries)
    other_queries = other_core(own_queries)

    def my_half(array):
        return lax.dynamic_slice_in_dim(array, core * HD, HD, 1)

    other_tokens = other_core(own_tokens)
    mine = my_half(kv_weight)
    others = my_half(other_weight)
    tall = 2 * rows
    spare = tall - (MAXDOC - 1) % (tall // BLK) * BLK
    short = tall - spare
    step_xy = ((spare, tall),)
    if slots == 4:

        def multiply(steps, sets, *rest, **more):
            return project((own_tokens, other_tokens), steps, sets, *rest, **more)

        def multiply_kept(steps, sets, *rest, **more):
            return project((kept,), steps, sets, *rest, **more)

        slab = jnp.concatenate([mine, others], axis=0)
        z3 = mirrored(slab)
        z1 = neighbours(slab)
        x0 = over_dp(slab, 1)
        y0 = over_dp(slab, 2)
        stacked, facts = stack(doc_blocks, block_mask, plan, own_queries, other_queries)
        slab, x0, y0, other_tokens, stacked, facts = tie(
            slab, x0, y0, other_tokens, stacked, facts
        )
        d0 = over_dp(x0, 2)
        x1 = over_dp(z1, 1)
        y1 = over_dp(z1, 2)
        z2 = neighbours(z3)
        z3, d0 = tie(z3, d0)
        x3 = over_dp(z3, 1)
        y3 = over_dp(z3, 2)
        half = slab.shape[0] // 2

        def diagonal(x, y):
            return over_dp(x[:half], 2), over_dp(y[half:], 1)

        own_sum, kept = multiply((0, 1, 3), [[slab, z1, z3]], last=False, keep=KEPT)
        d1 = over_dp(y1, 1)
        x2 = over_dp(z2, 1)
        y2 = over_dp(z2, 2)
        own_near = multiply_kept((2,), [[z2]], own_sum)
        own_back = around(own_near, 1)
        own_near, x3, y3 = tie(own_near, x3, y3)
        xy_sum = multiply((0, 1, 3), [[x0, x1, x3], [y0, y1, y3]], last=False)
        xy_sum, x2, y2, x3, y3 = tie(xy_sum, x2, y2, x3, y3)
        d2 = over_dp(x2, 2)
        d3 = diagonal(x3, y3)
        xy_near = multiply_kept(
            (2,), [[x2], [y2]], xy_sum, passed=step_xy, extra=own_back, cost=0
        )
        xy_back = around(xy_near, 1)
        d_sum = multiply((0,), [[d0]], last=False, cost=0)
        xy_far = around(xy_back[spare : 2 * tall], 1)
        d_near = multiply_kept((1, 2, 3), [[d1, d2, d3]], d_sum)
        d_back = around(d_near, 1)
        d_far = around(d_back[spare:], 1)
    else:
        stacked, facts = stack(doc_blocks, block_mask, plan, own_queries, other_queries)
        even = jnp.where(core == 0, mine, others)
        odd = jnp.where(core == 0, others, mine)
        groups = [list(range(0, size, 2)), list(range(1, size, 2))]
        slab = jnp.concatenate([even, odd], axis=0)
        own_set = lax.all_gather(slab, "ctx", axis=0, axis_index_groups=groups, tiled=True)
        pair_tokens = jnp.where(
            core == 0,
            jnp.concatenate([own_tokens, other_tokens], axis=0),
            jnp.concatenate([other_tokens, own_tokens], axis=0),
        )

        def multiply(sets, passed=(), extra=None):
            parts = [
                jnp.dot(pair_tokens, w, preferred_element_type=jnp.float32).astype(jnp.bfloat16)
                for w in sets
            ]
            parts += [extra[begin:end] for begin, end in passed]
            return jnp.concatenate(parts, axis=0)

        x_set = over_dp(own_set, 1)
        y_set = over_dp(own_set, 2)
        d_set = over_dp(x_set, 2)
        own_near = multiply([own_set])
        own_back = around(own_near, 1)
        xy_near = multiply([x_set, y_set], step_xy, own_back)
        xy_back = around(xy_near, 1)
        d_near = multiply([d_set])
        xy_far = around(xy_back[spare : 2 * tall], 1)
        d_back = around(d_near, 1)
        d_far = around(d_back[spare:], 1)

    own_set = (own_near, own_back, xy_back), (0, 0, 2 * tall)
    y_set = (xy_near, xy_back, xy_far), (tall, tall, tall)
    x_set = (xy_near, xy_back, xy_far), (0, 0, 0)
    d_set = (d_near, d_back, d_far), (0, 0, 0)
    near_a = attend_near(0, facts, stacked, own_set, y_set)
    near_b = attend_near(1, facts, stacked, x_set, d_set)
    first = attend_far(0, facts, stacked, near_a, own_set, y_set)
    second = attend_far(1, facts, stacked, near_b, x_set, d_set, first[2:])
    got_a, got_b = other_core(first[1]), other_core(second[1])
    st_got = other_core(second[3])
    vmem = pl.BlockSpec(memory_space=pltpu.VMEM)
    return pl.pallas_call(
        finish_kernel,
        out_shape=(
            jax.ShapeDtypeStruct((1, rows, QH * HD), jnp.bfloat16),
            jax.ShapeDtypeStruct((1, QH, rows), jnp.float32),
        ),
        in_specs=[vmem] * 6,
        out_specs=(vmem, vmem),
        compiler_params=pltpu.CompilerParams(vmem_limit_bytes=VMEM_LIMIT),
    )(first[0], second[0], got_a, got_b, second[2], st_got)


def solution(mesh):
    in_specs = (
        P("dp", "ctx", None),
        P("dp", "ctx", None),
        P("ctx", "dp"),
        P("dp", None),
        P("dp", None, None),
        P("dp", None),
    )
    out_specs = (P("dp", "ctx", None), P("dp", None, "ctx"))
    return jax.shard_map(body, mesh=mesh, in_specs=in_specs, out_specs=out_specs, check_vma=False)
```

```python
import functools
import math

import jax
import jax.numpy as jnp
from jax import lax
from jax.experimental import pallas as pl
from jax.experimental.pallas import tpu as pltpu
from jax.sharding import PartitionSpec as P

HD = 128
QH = 16
KVH = 4
BLK = 128
MAXDOC = 8
GROUP = QH // KVH
LANES = GROUP * BLK
KEPT = (1, 2, 3)
VMEM_LIMIT = 20 * 1024 * 1024
SCALE = 1.0 / math.sqrt(HD)
LOG2E = 1.0 / math.log(2.0)


def over_dp(array, mask):
    return lax.ppermute(array, "dp", [(i, i ^ mask) for i in range(lax.axis_size("dp"))])


def other_core(array):
    return lax.ppermute(array, "ctx", [(i, i ^ 1) for i in range(lax.axis_size("ctx"))])


def around(array, pairs):
    size = lax.axis_size("ctx")
    return lax.ppermute(array, "ctx", [(i, (i + 2 * pairs) % size) for i in range(size)])


def neighbours(array):
    return lax.ppermute(array, "ctx", [(i, i ^ 2) for i in range(lax.axis_size("ctx"))])


def mirrored(array):
    size = lax.axis_size("ctx")
    pairs = [(i, size - 2 - 2 * (i // 2) + i % 2) for i in range(size)]
    return lax.ppermute(array, "ctx", pairs)


def tie(*arrays):
    return lax.optimization_barrier(arrays)


def project_kernel(steps, sets, passed, has_sum, last, keep, depth, *refs):
    refs = list(refs)
    whole = keep is not None
    tokens = [refs.pop(0) for _ in range(2 if whole else 1)]
    weights = []
    for _ in range(len(steps) * sets):
        array = refs.pop(0)
        if array.shape[0] == depth:
            weights.append(((array, 0), (refs.pop(0), 0)))
        else:
            weights.append(((array, 0), (array, depth)))
    kept_ref = refs.pop() if keep else None
    out_ref = refs.pop()
    extras = refs
    device = lax.axis_index("ctx")
    core, pair = device % 2, device // 2
    rows = tokens[0].shape[0] // (1 if whole else 2)

    sources = (pair, pair + 1 - 2 * lax.rem(pair, 2), lax.rem(pair + 2, 4), 3 - pair)

    def group_columns(step, half):
        source = sources[step]
        group = 2 * source + (core + half) % 2
        return pl.ds(pl.multiple_of(group * depth, depth), depth)

    for side in range(2):
        place = core if side == 0 else 1 - core
        here = pl.ds(pl.multiple_of(place * rows, rows), rows)
        if has_sum:
            total = extras[0][here, :]
        else:
            total = jnp.zeros((rows, sets * HD), jnp.float32)
        for position, step in enumerate(steps):
            for half in range(2):
                if whole:
                    piece = tokens[side][:, group_columns(step, half)]
                else:
                    at = (2 * (step - KEPT[0]) + half) * depth
                    piece = tokens[0][side * rows : (side + 1) * rows, at : at + depth]
                parts = [weights[s * len(steps) + position][half] for s in range(sets)]
                weight = jnp.concatenate([array[at : at + depth, :] for array, at in parts], axis=1)
                total += jnp.dot(piece, weight, preferred_element_type=jnp.float32)
        for position, step in enumerate(keep or ()):
            for half in range(2):
                at = (2 * position + half) * depth
                kept_ref[side * rows : (side + 1) * rows, at : at + depth] = tokens[side][
                    :, group_columns(step, half)
                ]
        if not last:
            out_ref[here, :] = total
            continue
        total = total.astype(jnp.bfloat16)
        for s in range(sets):
            at = pl.multiple_of(s * 2 * rows + place * rows, rows)
            out_ref[pl.ds(at, rows), :] = total[:, s * HD : (s + 1) * HD]
    at = sets * 2 * rows
    for begin, end in passed:
        out_ref[at : at + end - begin, :] = extras[-1][begin:end, :]
        at += end - begin


def project(
    tokens, steps, sets, total=None, last=True, passed=(), extra=None, keep=(), cost=1
):
    whole = len(tokens) == 2
    rows = tokens[0].shape[0] * len(tokens)
    weights = []
    for one in sets:
        for w in one:
            weights += w if isinstance(w, tuple) else [w]
    first = sets[0][0]
    depth = first[0].shape[0] if isinstance(first, tuple) else first.shape[0] // 2
    extras = [array for array in (total, extra) if array is not None]
    count = len(sets)
    tall = count * rows + sum(end - begin for begin, end in passed)
    if last:
        out = [jax.ShapeDtypeStruct((tall, HD), jnp.bfloat16)]
    else:
        out = [jax.ShapeDtypeStruct((rows, count * HD), jnp.float32)]
    if keep:
        out.append(jax.ShapeDtypeStruct((rows, len(keep) * 2 * depth), jnp.bfloat16))
    spec = pl.BlockSpec(memory_space=pltpu.VMEM)
    got = pl.pallas_call(
        functools.partial(
            project_kernel,
            steps,
            count,
            passed,
            total is not None,
            last,
            keep if whole else None,
            depth,
        ),
        out_shape=tuple(out),
        in_specs=[spec] * (len(tokens) + len(weights) + len(extras)),
        out_specs=(spec,) * len(out),
        compiler_params=pltpu.CompilerParams(vmem_limit_bytes=VMEM_LIMIT),
        cost_estimate=pl.CostEstimate(
            flops=4 * rows * depth * HD * len(steps) * count * cost,
            bytes_accessed=4 * rows * depth * len(steps) * cost,
            transcendentals=0,
        ),
    )(*tokens, *weights, *extras)
    return got if keep else got[0]


def document_start(docs_ref, block):
    def ends(j, carry):
        end, start = carry
        end = end + docs_ref[0, j]
        return end, jnp.where(end <= block, end, start)

    return lax.fori_loop(0, docs_ref.shape[1], ends, (jnp.int32(0), jnp.int32(0)))[1]


def score_blocks(keys, query, steps, found, causal, table):
    got = lax.dot_general(
        jnp.concatenate([keys(step) for step in steps], axis=0),
        query,
        (((1,), (1,)), ((), ())),
        preferred_element_type=jnp.float32,
    )
    best = None
    for at, step in enumerate(steps):
        part = got[at * BLK : (at + 1) * BLK, :]
        keep = causal if step == 0 and causal is not None else step < found
        part = jnp.where(keep, part, -jnp.inf)
        table[step * BLK : (step + 1) * BLK, :] = part
        best = part if best is None else jnp.maximum(best, part)
    return jnp.max(best, axis=0, keepdims=True)


def weigh_blocks(values, steps, highest, table):
    weights = jnp.exp2(
        (table[steps[0] * BLK : (steps[-1] + 1) * BLK, :] - highest) * (SCALE * LOG2E)
    )
    part = lax.dot_general(
        jnp.concatenate([values(step) for step in steps], axis=0),
        weights.astype(jnp.bfloat16),
        (((0,), (0,)), ((), ())),
        preferred_element_type=jnp.float32,
    )
    return jnp.sum(weights, axis=0, keepdims=True), part


def where_am_i(second):
    device = lax.axis_index("ctx")
    slice_of = lax.axis_index("dp")
    core, pair = device % 2, device // 2
    column, kind = slice_of % 2, slice_of // 2
    return core, pair, kind, 2 * ((column + second) % 2) + core


def stack_kernel(docs_ref, mask_ref, plan_ref, q_own_ref, q_other_ref, out_ref, facts):
    core, pair, _, _ = where_am_i(0)
    blocks = q_own_ref.shape[0] // BLK
    for side in range(2):
        for place in range(blocks):
            item = side * blocks + place
            index = (core if side == 0 else 1 - core) * blocks + place
            block = 2 * blocks * pair + index
            start = document_start(docs_ref, block)
            for back in range(1, MAXDOC):
                admitted = jnp.logical_and(
                    block - back >= start, mask_ref[0, block, back - 1] == 1
                )
                facts[item, back] = admitted.astype(jnp.int32)
            facts[item, 0] = index
            facts[item, MAXDOC] = plan_ref[0, block] - 2 * blocks * pair
    for second in range(2):
        head = where_am_i(second)[3]
        columns = pl.ds(pl.multiple_of(head * LANES, LANES), LANES)
        for side, q_ref in enumerate((q_own_ref, q_other_ref)):
            for place in range(blocks):
                query = q_ref[place * BLK : (place + 1) * BLK, columns]
                for g in range(GROUP):
                    out_ref[second, side * blocks + place, g * BLK : (g + 1) * BLK, :] = query[
                        :, g * HD : (g + 1) * HD
                    ]


def stack(docs, mask, plan, q_own, q_other):
    vmem = pl.BlockSpec(memory_space=pltpu.VMEM)
    smem = pl.BlockSpec(memory_space=pltpu.SMEM)
    items = 2 * q_own.shape[0] // BLK
    return pl.pallas_call(
        stack_kernel,
        out_shape=(
            jax.ShapeDtypeStruct((2, items, LANES, HD), jnp.bfloat16),
            jax.ShapeDtypeStruct((items, MAXDOC + 1), jnp.int32),
        ),
        in_specs=[smem] * 3 + [vmem] * 2,
        out_specs=(vmem, smem),
        compiler_params=pltpu.CompilerParams(vmem_limit_bytes=VMEM_LIMIT),
        cost_estimate=pl.CostEstimate(
            flops=0, bytes_accessed=4 * items * LANES * HD, transcendentals=0
        ),
    )(docs, mask, plan, q_own, q_other)


def near_kernel(
    second,
    starts,
    facts,
    queries_ref,
    near_a,
    near_b,
    back_a,
    back_b,
    summed,
    stat,
    kv,
    table,
    places,
):
    kind = where_am_i(second)[2]
    pair_blocks = queries_ref.shape[1]
    tall = pair_blocks * BLK
    for which, near, back, at in (
        (kind, near_a, back_a, starts[0]),
        (1 - kind, near_b, back_b, starts[1]),
    ):
        kv[which, :tall, :] = back[at[1] : at[1] + tall, :]
        kv[which, tall:, :] = near[at[0] : at[0] + tall, :]
    causal = lax.broadcasted_iota(jnp.int32, (BLK, BLK), 0) <= lax.broadcasted_iota(
        jnp.int32, (BLK, BLK), 1
    )
    causal = jnp.tile(causal, (1, GROUP))

    for item in range(pair_blocks):
        index = facts[item, 0]
        for step in range(MAXDOC + 1):
            places[step] = tall + index * BLK
        found = jnp.int32(1)
        for back in range(1, MAXDOC):
            places[found] = tall + (index - back) * BLK
            found += jnp.where(back <= index + pair_blocks, facts[item, back], 0)
        places[found] = tall + index * BLK
        rows = queries_ref[second, item]

        def fetch(which, step):
            return kv[which, pl.ds(pl.multiple_of(places[step], BLK), BLK), :]

        keys = functools.partial(fetch, 0)
        values = functools.partial(fetch, 1)
        half = MAXDOC // 2
        low, high = range(half), range(half, MAXDOC)
        stat[item, 0:1, :] = score_blocks(keys, rows, low, found, causal, table)

        few = jnp.logical_and(found > half, found <= half + 2)
        many = found > half + 2

        def score_rest(steps):
            stat[item, 0:1, :] = jnp.maximum(
                stat[item, 0:1, :], score_blocks(keys, rows, steps, found, None, table)
            )

        def weigh_rest(steps):
            more, part = weigh_blocks(values, steps, stat[item, 0:1, :], table)
            stat[item, 1:2, :] += more
            summed[item] += part

        pl.when(few)(functools.partial(score_rest, high[:2]))
        pl.when(many)(functools.partial(score_rest, high))
        stat[item, 1:2, :], summed[item] = weigh_blocks(values, low, stat[item, 0:1, :], table)

        pl.when(few)(functools.partial(weigh_rest, high[:2]))
        pl.when(many)(functools.partial(weigh_rest, high))


def far_kernel(
    second,
    starts,
    facts,
    summed_ref,
    stat_ref,
    queries_ref,
    far_a,
    far_b,
    *refs,
):
    before_own, before_other = refs[:2] if second else (None, None)
    (
        out_own,
        out_other,
        stats_own,
        stats_other,
        kv,
        table,
        top,
        total,
        summed,
        places,
    ) = refs[2 * second :]
    core, _, kind, _ = where_am_i(second)
    if second:
        dev = before_own.shape[0]
        stats_own[dev:, :, :] = before_own[...]
        stats_other[dev:, :, :] = before_other[...]
    pair_blocks = queries_ref.shape[1]
    dev_blocks = pair_blocks // 2
    far_blocks = (MAXDOC - 1) % pair_blocks
    short = far_blocks * BLK
    for which, far, at in ((kind, far_a, starts[0]), (1 - kind, far_b, starts[1])):
        kv[which, :, :] = far[at[2] : at[2] + short, :]

    for item in range(pair_blocks):
        side, place = divmod(item, dev_blocks)
        out_ref = (out_own, out_other)[side]
        rows = slice(place * BLK, (place + 1) * BLK)
        index = facts[item, 0]
        for step in range(far_blocks + 1):
            places[step] = 0
        found = jnp.int32(0)
        for back in range(MAXDOC - far_blocks, MAXDOC):
            places[found] = (far_blocks + pair_blocks + index - back) * BLK
            found += jnp.where(back > index + pair_blocks, facts[item, back], 0)
        places[found] = 0
        top[...] = stat_ref[item, 0:1, :]
        total[...] = stat_ref[item, 1:2, :]
        summed[...] = summed_ref[item]

        @pl.when(found > 0)
        def _():
            query = queries_ref[second, item]

            def fetch(which, step):
                return kv[which, pl.ds(pl.multiple_of(places[step], BLK), BLK), :]

            steps = range(far_blocks)
            before = top[...]
            highest = jnp.maximum(
                before,
                score_blocks(functools.partial(fetch, 0), query, steps, found, None, table),
            )
            more, part = weigh_blocks(functools.partial(fetch, 1), steps, highest, table)
            shrink = jnp.exp2((before - highest) * (SCALE * LOG2E))
            top[...] = highest
            total[...] = total[...] * shrink + more
            summed[...] = summed[...] * shrink + part

        result = summed[...] / total[...]
        for g in range(GROUP):
            out_ref[rows, g * HD : (g + 1) * HD] = (
                result[:, g * BLK : (g + 1) * BLK].T.astype(jnp.bfloat16)
            )
        lse = top[...] * SCALE + jnp.log(total[...])
        slot = facts[item, MAXDOC]
        keep_here = slot // dev_blocks == core
        slot_at = slot % dev_blocks

        @pl.when(keep_here)
        def _():
            for g in range(GROUP):
                stats_own[slot_at, g : g + 1, :] = lse[:, g * BLK : (g + 1) * BLK]

        @pl.when(jnp.logical_not(keep_here))
        def _():
            for g in range(GROUP):
                stats_other[slot_at, g : g + 1, :] = lse[:, g * BLK : (g + 1) * BLK]


def attend_near(second, facts, queries, first_set, second_set):
    vmem = pl.BlockSpec(memory_space=pltpu.VMEM)
    smem = pl.BlockSpec(memory_space=pltpu.SMEM)
    items = queries.shape[1]
    (near_a, back_a, _), start_a = first_set
    (near_b, back_b, _), start_b = second_set
    return pl.pallas_call(
        functools.partial(near_kernel, second, (start_a, start_b)),
        out_shape=(
            jax.ShapeDtypeStruct((items, HD, LANES), jnp.float32),
            jax.ShapeDtypeStruct((items, 8, LANES), jnp.float32),
        ),
        in_specs=[smem] + [vmem] * 5,
        out_specs=(vmem,) * 2,
        scratch_shapes=[
            pltpu.VMEM((2, 2 * items * BLK, HD), jnp.bfloat16),
            pltpu.VMEM((MAXDOC * BLK, LANES), jnp.float32),
            pltpu.SMEM((MAXDOC + 1,), jnp.int32),
        ],
        compiler_params=pltpu.CompilerParams(vmem_limit_bytes=VMEM_LIMIT),
        cost_estimate=pl.CostEstimate(
            flops=items * MAXDOC * BLK * LANES * HD * 4,
            bytes_accessed=4 * items * BLK * QH * HD,
            transcendentals=items * MAXDOC * BLK * LANES,
        ),
    )(facts, queries, near_a, near_b, back_a, back_b)


def attend_far(second, facts, queries, carried, first_set, second_set, before=()):
    vmem = pl.BlockSpec(memory_space=pltpu.VMEM)
    smem = pl.BlockSpec(memory_space=pltpu.SMEM)
    items = queries.shape[1]
    dev_blocks = items // 2
    rows = dev_blocks * BLK
    far_blocks = (MAXDOC - 1) % items
    (_, _, far_a), start_a = first_set
    (_, _, far_b), start_b = second_set
    out = jax.ShapeDtypeStruct((rows, LANES), jnp.bfloat16)
    stats = jax.ShapeDtypeStruct(((1 + second) * dev_blocks, GROUP, BLK), jnp.float32)
    return pl.pallas_call(
        functools.partial(far_kernel, second, (start_a, start_b)),
        out_shape=(out, out, stats, stats),
        in_specs=[smem] + [vmem] * (5 + len(before)),
        out_specs=(vmem,) * 4,
        scratch_shapes=[
            pltpu.VMEM((2, far_blocks * BLK, HD), jnp.bfloat16),
            pltpu.VMEM((far_blocks * BLK, LANES), jnp.float32),
            pltpu.VMEM((1, LANES), jnp.float32),
            pltpu.VMEM((1, LANES), jnp.float32),
            pltpu.VMEM((HD, LANES), jnp.float32),
            pltpu.SMEM((far_blocks + 1,), jnp.int32),
        ],
        compiler_params=pltpu.CompilerParams(vmem_limit_bytes=VMEM_LIMIT),
        cost_estimate=pl.CostEstimate(
            flops=items * far_blocks * BLK * LANES * HD * 4,
            bytes_accessed=8 * rows * LANES,
            transcendentals=items * far_blocks * BLK * LANES,
        ),
    )(facts, *carried, queries, far_a, far_b, *before)


def finish_kernel(own_a, own_b, got_a, got_b, st_own, st_got, out_ref, stats_ref):
    core = lax.axis_index("ctx") % 2
    column = lax.axis_index("dp") % 2
    pieces = (
        (own_a, column, core),
        (own_b, 1 - column, core),
        (got_a, column, 1 - core),
        (got_b, 1 - column, 1 - core),
    )
    for piece, head_pair, side in pieces:
        head = 2 * head_pair + side
        out_ref[0, :, pl.ds(pl.multiple_of(head * LANES, LANES), LANES)] = piece[...]
    for head in range(KVH):
        is_a = head // 2 == column
        is_own = head % 2 == core
        both = jnp.where(is_own, st_own[...], st_got[...])
        lse = jnp.where(is_a, both[both.shape[0] // 2 :], both[: both.shape[0] // 2])
        for place in range(lse.shape[0]):
            stats_ref[0, head * GROUP : (head + 1) * GROUP, place * BLK : (place + 1) * BLK] = lse[place]


def body(tokens, queries, kv_weight, doc_blocks, block_mask, plan):
    size = lax.axis_size("ctx")
    device = lax.axis_index("ctx")
    core = device % 2
    slots = size // 2
    own_tokens, own_queries = tokens[0], queries[0]
    rows = own_tokens.shape[0]
    other_weight = other_core(kv_weight)
    other_weight, own_tokens, own_queries = tie(other_weight, own_tokens, own_queries)
    other_queries = other_core(own_queries)

    def my_half(array):
        return lax.dynamic_slice_in_dim(array, core * HD, HD, 1)

    other_tokens = other_core(own_tokens)
    mine = my_half(kv_weight)
    others = my_half(other_weight)
    tall = 2 * rows
    spare = tall - (MAXDOC - 1) % (tall // BLK) * BLK
    short = tall - spare
    step_xy = ((spare, tall),)
    if slots == 4:

        def multiply(steps, sets, *rest, **more):
            return project((own_tokens, other_tokens), steps, sets, *rest, **more)

        def multiply_kept(steps, sets, *rest, **more):
            return project((kept,), steps, sets, *rest, **more)

        slab = jnp.concatenate([mine, others], axis=0)
        z3 = mirrored(slab)
        z1 = neighbours(slab)
        x0 = over_dp(slab, 1)
        y0 = over_dp(slab, 2)
        stacked, facts = stack(doc_blocks, block_mask, plan, own_queries, other_queries)
        slab, x0, y0, other_tokens, stacked, facts = tie(
            slab, x0, y0, other_tokens, stacked, facts
        )
        d0 = over_dp(x0, 2)
        x1 = over_dp(z1, 1)
        y1 = over_dp(z1, 2)
        z2 = neighbours(z3)
        z3, d0 = tie(z3, d0)
        x3 = over_dp(z3, 1)
        y3 = over_dp(z3, 2)
        half = slab.shape[0] // 2

        def diagonal(x, y):
            return over_dp(x[:half], 2), over_dp(y[half:], 1)

        own_sum, kept = multiply((0, 1, 3), [[slab, z1, z3]], last=False, keep=KEPT)
        d1 = over_dp(y1, 1)
        x2 = over_dp(z2, 1)
        y2 = over_dp(z2, 2)
        own_near = multiply_kept((2,), [[z2]], own_sum)
        own_back = around(own_near, 1)
        own_near, x3, y3 = tie(own_near, x3, y3)
        xy_sum = multiply((0, 1, 3), [[x0, x1, x3], [y0, y1, y3]], last=False)
        xy_sum, x2, y2, x3, y3 = tie(xy_sum, x2, y2, x3, y3)
        d2 = over_dp(x2, 2)
        d3 = diagonal(x3, y3)
        xy_near = multiply_kept(
            (2,), [[x2], [y2]], xy_sum, passed=step_xy, extra=own_back, cost=0
        )
        xy_back = around(xy_near, 1)
        d_sum = multiply((0,), [[d0]], last=False, cost=0)
        xy_far = around(xy_back[spare : 2 * tall], 1)
        d_near = multiply_kept((1, 2, 3), [[d1, d2, d3]], d_sum)
        d_back = around(d_near, 1)
        d_far = around(d_near[spare:], 2)
    else:
        stacked, facts = stack(doc_blocks, block_mask, plan, own_queries, other_queries)
        even = jnp.where(core == 0, mine, others)
        odd = jnp.where(core == 0, others, mine)
        groups = [list(range(0, size, 2)), list(range(1, size, 2))]
        slab = jnp.concatenate([even, odd], axis=0)
        own_set = lax.all_gather(slab, "ctx", axis=0, axis_index_groups=groups, tiled=True)
        pair_tokens = jnp.where(
            core == 0,
            jnp.concatenate([own_tokens, other_tokens], axis=0),
            jnp.concatenate([other_tokens, own_tokens], axis=0),
        )

        def multiply(sets, passed=(), extra=None):
            parts = [
                jnp.dot(pair_tokens, w, preferred_element_type=jnp.float32).astype(jnp.bfloat16)
                for w in sets
            ]
            parts += [extra[begin:end] for begin, end in passed]
            return jnp.concatenate(parts, axis=0)

        x_set = over_dp(own_set, 1)
        y_set = over_dp(own_set, 2)
        d_set = over_dp(x_set, 2)
        own_near = multiply([own_set])
        own_back = around(own_near, 1)
        xy_near = multiply([x_set, y_set], step_xy, own_back)
        xy_back = around(xy_near, 1)
        d_near = multiply([d_set])
        xy_far = around(xy_back[spare : 2 * tall], 1)
        d_back = around(d_near, 1)
        d_far = around(d_near[spare:], 2)

    own_set = (own_near, own_back, xy_back), (0, 0, 2 * tall)
    y_set = (xy_near, xy_back, xy_far), (tall, tall, tall)
    x_set = (xy_near, xy_back, xy_far), (0, 0, 0)
    d_set = (d_near, d_back, d_far), (0, 0, 0)
    near_a = attend_near(0, facts, stacked, own_set, y_set)
    near_b = attend_near(1, facts, stacked, x_set, d_set)
    first = attend_far(0, facts, stacked, near_a, own_set, y_set)
    second = attend_far(1, facts, stacked, near_b, x_set, d_set, first[2:])
    got_a, got_b = other_core(first[1]), other_core(second[1])
    st_got = other_core(second[3])
    vmem = pl.BlockSpec(memory_space=pltpu.VMEM)
    return pl.pallas_call(
        finish_kernel,
        out_shape=(
            jax.ShapeDtypeStruct((1, rows, QH * HD), jnp.bfloat16),
            jax.ShapeDtypeStruct((1, QH, rows), jnp.float32),
        ),
        in_specs=[vmem] * 6,
        out_specs=(vmem, vmem),
        compiler_params=pltpu.CompilerParams(vmem_limit_bytes=VMEM_LIMIT),
    )(first[0], second[0], got_a, got_b, second[2], st_got)


def solution(mesh):
    in_specs = (
        P("dp", "ctx", None),
        P("dp", "ctx", None),
        P("ctx", "dp"),
        P("dp", None),
        P("dp", None, None),
        P("dp", None),
    )
    out_specs = (P("dp", "ctx", None), P("dp", None, "ctx"))
    return jax.shard_map(body, mesh=mesh, in_specs=in_specs, out_specs=out_specs, check_vma=False)
```
